32 devices in a mesh: rows: 8 (over z, y), feat: 4 (over x, core).
Axes of the slice: x: 2, y: 2, z: 4, core: 2. Of those that a mesh axis runs over, the one named last changes fastest.
Arguments:
- inputs: bfloat16 [8, 48, 256, 512], P('rows', 'feat'), may hold values from -6 to 6
- feat_gain: bfloat16 [512], P(('rows', 'feat')), may hold values from 0.5 to 1.5
- feat_shift: bfloat16 [512], P(('rows', 'feat')), may hold values from -3 to 3
- feat_qkv: bfloat16 [512, 1536], P(('rows', 'feat')), may hold values from -0.25 to 0.25
- feat_out: bfloat16 [512, 512], P(('rows', 'feat')), may hold values from -0.75 to 0.75
- row_gain: bfloat16 [512], P(('rows', 'feat')), may hold values from 0.5 to 1.5
- row_shift: bfloat16 [512], P(('rows', 'feat')), may hold values from -3 to 3
- row_qkv: bfloat16 [512, 1536], P(('rows', 'feat')), may hold values from -0.25 to 0.25
- row_out: bfloat16 [512, 512], P(('rows', 'feat')), may hold values from -0.75 to 0.75
- mlp_gain: bfloat16 [512], P(('rows', 'feat')), may hold values from 0.5 to 1.5
- mlp_shift: bfloat16 [512], P(('rows', 'feat')), may hold values from -3 to 3
- mlp_in: bfloat16 [512, 2048], P(('rows', 'feat')), may hold values from -0.25 to 0.25
- mlp_out: bfloat16 [2048, 512], P(('rows', 'feat')), may hold values from -0.125 to 0.125
- cotangent: bfloat16 [8, 48, 256, 512], P('rows', 'feat'), may hold values from -6 to 6
- segments: int32 [8, 256], P('rows'), may hold values from 0 to 3, as said below
- context: int32 [8, 4], P('rows'), may hold values from 1 to 96, as said below
- feature_mask: int32 [8, 48], P('rows'), may hold values from 0 to 1, as said below
Outputs:
- output: bfloat16 [8, 48, 256, 512], P('rows', 'feat')
- input_grad: float32 [8, 48, 256, 512], P('rows', 'feat')
- feat_gain_grad: float32 [512], P(('rows', 'feat'))
- feat_shift_grad: float32 [512], P(('rows', 'feat'))
- feat_qkv_grad: float32 [512, 1536], P(('rows', 'feat'))
- feat_out_grad: float32 [512, 512], P(('rows', 'feat'))
- row_gain_grad: float32 [512], P(('rows', 'feat'))
- row_shift_grad: float32 [512], P(('rows', 'feat'))
- row_qkv_grad: float32 [512, 1536], P(('rows', 'feat'))
- row_out_grad: float32 [512, 512], P(('rows', 'feat'))
- mlp_gain_grad: float32 [512], P(('rows', 'feat'))
- mlp_shift_grad: float32 [512], P(('rows', 'feat'))
- mlp_in_grad: float32 [512, 2048], P(('rows', 'feat'))
- mlp_out_grad: float32 [2048, 512], P(('rows', 'feat'))
The draws below stay inside these ranges and needn't reach their ends.
Inputs may be any that keep to these rules, and one draw needn't show every extreme that they name: `segments`: within a slot table numbers never fall along the rows and every table has at least one row. `context`: each table's count is at most its number of rows. `feature_mask`: feature 0 of every slot is real.
All inputs are finite; a program needn't handle non-finite values.
Results may differ from the reference program's by a relative error of at most 0.018.
Values may be sent and summed in bfloat16 or wider, within the bound.
No kernel may reach another device: no remote copies, remote signals or barrier semaphores. Data moves between devices by JAX's collectives and lax.ppermute only.
A program may use at most 320 MiB of HBM per device.

```python
import jax
import jax.numpy as jnp
from jax import lax

D = 512
HEADS = 4
HEAD_DIM = 128
FF = 2048
FEATS = 48
ROWS_SLOT = 256
TABLES = 4
SLOTS = 8


def table_bounds(key):
    stride = ROWS_SLOT // TABLES
    jitter = stride // 4
    offsets = jax.random.randint(key, (SLOTS, TABLES - 1), -jitter, jitter + 1)
    if TABLES >= 3:
        offsets = offsets.at[0, 0].set(-jitter)
        offsets = offsets.at[0, 1].set(jitter)
    else:
        offsets = offsets.at[0, 0].set(jitter)
    return stride * jnp.arange(1, TABLES, dtype=jnp.int32)[None, :] + offsets


def draw_segments(key, part):
    boundaries = table_bounds(key)
    places = jnp.arange(ROWS_SLOT, dtype=jnp.int32)
    return jnp.sum((places[None, :, None] >= boundaries[:, None, :]).astype(jnp.int32), axis=2)


def draw_context(key, part):
    boundaries = table_bounds(key)
    key = jax.random.fold_in(key, 6)
    edges = jnp.concatenate((jnp.zeros((SLOTS, 1), jnp.int32), boundaries, jnp.full((SLOTS, 1), ROWS_SLOT, jnp.int32)), axis=1)
    table_sizes = edges[:, 1:] - edges[:, :-1]
    counts = jax.random.randint(key, (SLOTS, TABLES), 1, table_sizes + 1)
    widest = 1 if TABLES >= 3 else 0
    counts = counts.at[0, widest].set(table_sizes[0, widest])
    return counts.at[0, TABLES - 1].set(1)


def draw_feature_mask(key, part):
    key = jax.random.fold_in(key, 7)
    keeping = (jax.random.randint(key, (SLOTS, FEATS), 0, 8) < 7).astype(jnp.int32)
    return keeping.at[:, 0].set(1)


def with_spikes(array, key, source, target, shards_of, factor):
    def block_of(dim):
        return (jnp.arange(array.shape[dim]) // (array.shape[dim] // shards_of)).reshape((-1,) + (1,) * (array.ndim - 1 - dim))

    near = jax.random.permutation(key, shards_of)[block_of(target)]
    second = (block_of(target) + shards_of // 2) % shards_of
    return jnp.where((block_of(source) == near) | (block_of(source) == second), factor * array, array)


def shard_levels(rng, shape, split, least, high):
    factor_of = 1.0
    for position, shards_of in split:
        draws = jax.random.uniform(jax.random.fold_in(jax.random.fold_in(rng, 6), position), (shards_of,), jnp.float32, least / len(split), high / len(split))
        factor_of = factor_of * jnp.repeat(jnp.exp(draws), shape[position] // shards_of).reshape((-1,) + (1,) * (len(shape) - 1 - position))
    return factor_of


def bell_draw(stream_key, extent, width, most, shards=(), held_as=jnp.bfloat16):
    entries = width * jax.random.normal(stream_key, extent, jnp.float32)
    if shards:
        entries = entries * shard_levels(stream_key, extent, shards, -0.22, 0.18)
    return jnp.clip(entries, -most, most).astype(held_as)


def bell_draw_with(rng, extent, width, limit, split, heavy, held_as=jnp.bfloat16):
    values = width * jax.random.normal(rng, extent, jnp.float32)
    if split:
        values = values * shard_levels(rng, extent, split, -0.22, 0.18)
    return jnp.clip(with_spikes(values, jax.random.fold_in(rng, 3), *heavy), -limit, limit).astype(held_as)


def setup_inputs(seed: int = 0) -> dict:
    key_list = jax.random.split(jax.random.key(seed), 18)
    return {
        "inputs": bell_draw(key_list[0], (SLOTS, FEATS, ROWS_SLOT, D), 1.0, 6.0, ((0, 8), (1, 4))),
        "feat_gain": jnp.clip(1.0 + 0.1 * jax.random.normal(key_list[1], (D,), jnp.float32), 0.5, 1.5).astype(jnp.bfloat16),
        "feat_shift": bell_draw(key_list[2], (D,), 0.5, 3.0, ((0, 32),)),
        "feat_qkv": bell_draw(key_list[3], (D, 3 * D), D ** -0.5, 0.25, ((0, 32),)),
        "feat_out": bell_draw(key_list[4], (D, D), (D // 8) ** -0.5, 0.75, ((0, 32),)),
        "row_gain": jnp.clip(1.0 + 0.1 * jax.random.normal(key_list[5], (D,), jnp.float32), 0.5, 1.5).astype(jnp.bfloat16),
        "row_shift": bell_draw(key_list[6], (D,), 0.5, 3.0, ((0, 32),)),
        "row_qkv": bell_draw(key_list[7], (D, 3 * D), D ** -0.5, 0.25, ((0, 32),)),
        "row_out": bell_draw(key_list[8], (D, D), (D // 8) ** -0.5, 0.75, ((0, 32),)),
        "mlp_gain": jnp.clip(1.0 + 0.1 * jax.random.normal(key_list[9], (D,), jnp.float32), 0.5, 1.5).astype(jnp.bfloat16),
        "mlp_shift": bell_draw(key_list[10], (D,), 0.5, 3.0, ((0, 32),)),
        "mlp_in": bell_draw(key_list[11], (D, FF), D ** -0.5, 0.25, ((0, 32),)),
        "mlp_out": bell_draw(key_list[12], (FF, D), FF ** -0.5, 0.125, ((0, 32),)),
        "cotangent": bell_draw_with(key_list[13], (SLOTS, FEATS, ROWS_SLOT, D), 1.0, 6.0, ((0, 8), (1, 4)), (0, 3, 8, 2.0)),
        "segments": draw_segments(jax.random.fold_in(key_list[17], 71), 0),
        "context": draw_context(jax.random.fold_in(key_list[17], 71), 0),
        "feature_mask": draw_feature_mask(jax.random.fold_in(key_list[17], 71), 0),
    }


@jax.custom_vjp
def low(v):
    return lax.optimization_barrier(v.astype(jnp.bfloat16)).astype(jnp.float32)

@jax.custom_vjp
def low_back(v):
    return v

def low_keep(v):
    return (low(v), None)

def low_pass(kept, grad):
    return (grad,)

def back_keep(v):
    return (v, None)

def back_low(kept, grad):
    return (low(grad),)
low.defvjp(low_keep, low_pass)
low_back.defvjp(back_keep, back_low)
precise = lax.Precision.HIGHEST
epsilon = 1e-05
masked_score = -1000000000.0

def layer_norm(hidden, scales, shifts):
    average = lax.optimization_barrier(jnp.mean(hidden, axis=-1, keepdims=True))
    centred = hidden - average
    spread = lax.optimization_barrier(jnp.mean(centred * centred, axis=-1, keepdims=True))
    return centred * lax.rsqrt(spread + epsilon) * scales + shifts

def row_allowed(segments, context):
    tables = jnp.arange(context.shape[0], dtype=jnp.int32)
    member = (segments[:, None] == tables[None, :]).astype(jnp.int32)
    table_sizes = lax.optimization_barrier(jnp.sum(member, axis=0))
    starts = jnp.cumsum(table_sizes) - table_sizes
    places = jnp.arange(segments.shape[0], dtype=jnp.int32) - lax.optimization_barrier(jnp.sum(member * starts[None, :], axis=1))
    limits = lax.optimization_barrier(jnp.sum(member * context[None, :], axis=1))
    usable = places < limits
    return (segments[:, None] == segments[None, :]) & usable[None, :]

def attend(queries, key_vecs, values, allowed, score_form, mix_form):
    scores = low_back(jnp.einsum(score_form, queries, key_vecs, precision=precise) * HEAD_DIM ** (-0.5))
    scores = jnp.where(allowed, scores, masked_score)
    highest = lax.optimization_barrier(jnp.max(scores, axis=-1, keepdims=True))
    weights = jnp.exp(scores - highest)
    attention = low(weights / lax.optimization_barrier(jnp.sum(weights, axis=-1, keepdims=True)))
    return jnp.einsum(mix_form, attention, values, precision=precise)

def project(values, weight):
    return jnp.einsum('frd,de->fre', values, weight, precision=precise)

def split_heads(packed):
    shaped = packed.reshape(packed.shape[0], packed.shape[1], 3, HEADS, HEAD_DIM)
    return (shaped[:, :, 0], shaped[:, :, 1], shaped[:, :, 2])

def block_layer(slot_in, params, feat_valid, allowed):
    feat_gain, feat_shift, feat_qkv, feat_out, row_gain, row_shift, row_qkv, row_out, mlp_gain, mlp_shift, mlp_in, mlp_out = params
    normed = low(layer_norm(slot_in, feat_gain, feat_shift))
    queries, key_vecs, values = split_heads(low_back(low(project(normed, feat_qkv))))
    mixture = attend(queries, key_vecs, values, feat_valid[None, None, None, :], 'frhd,grhd->rhfg', 'rhfg,grhd->frhd')
    mixture = low_back(low(mixture.reshape(slot_in.shape)))
    after_feat = slot_in + low_back(project(mixture, feat_out))
    normed = low(layer_norm(after_feat, row_gain, row_shift))
    queries, key_vecs, values = split_heads(low_back(low(project(normed, row_qkv))))
    mixture = attend(queries, key_vecs, values, allowed[None, None], 'frhd,fthd->fhrt', 'fhrt,fthd->frhd')
    mixture = low_back(low(mixture.reshape(slot_in.shape)))
    after_row = after_feat + low_back(project(mixture, row_out))
    normed = low(layer_norm(after_row, mlp_gain, mlp_shift))
    hidden = low_back(jnp.einsum('frd,de->fre', normed, mlp_in, precision=precise))
    active = low(jax.nn.gelu(hidden, approximate=False))
    return after_row + low_back(jnp.einsum('fre,ed->frd', active, mlp_out, precision=precise))

def reference(inputs, feat_gain, feat_shift, feat_qkv, feat_out, row_gain, row_shift, row_qkv, row_out, mlp_gain, mlp_shift, mlp_in, mlp_out, cotangent, segments, context, feature_mask):
    params = tuple((weight.astype(jnp.float32) for weight in (feat_gain, feat_shift, feat_qkv, feat_out, row_gain, row_shift, row_qkv, row_out, mlp_gain, mlp_shift, mlp_in, mlp_out)))

    def one_slot(totals, slot_data):
        slot_in, slot_cot, slot_seg, slot_ctx, slot_mask = slot_data
        allowed = row_allowed(slot_seg, slot_ctx)

        def forward(hidden, weights):
            return block_layer(hidden, weights, slot_mask > 0, allowed)
        result, pullback = jax.vjp(forward, slot_in.astype(jnp.float32), params)
        slot_grad, param_grads = pullback(slot_cot.astype(jnp.float32))
        totals = jax.tree.map(lambda earlier, later: earlier + later, totals, param_grads)
        return (totals, (result.astype(jnp.bfloat16), slot_grad))
    starting = jax.tree.map(jnp.zeros_like, params)
    param_sums, (outputs, input_grads) = lax.scan(one_slot, starting, (inputs, cotangent, segments, context, feature_mask))
    return (outputs, input_grads, param_sums[0], param_sums[1], param_sums[2], param_sums[3], param_sums[4], param_sums[5], param_sums[6], param_sums[7], param_sums[8], param_sums[9], param_sums[10], param_sums[11])
```

```python
import jax
import jax.numpy as jnp
import numpy as np
from jax import lax
from jax.experimental import pallas as pl
from jax.experimental.pallas import tpu as pltpu
from jax.sharding import PartitionSpec as P

D = 512
HEADS = 4
HEAD_DIM = 128
FF = 2048
QKV = 3 * D
EPS = 1e-05
MASKED = -1e30
SCALE = HEAD_DIM**-0.5
BF = jnp.bfloat16
F32 = jnp.float32
LOG2E = float(np.log2(np.e))
VMEM = 60 * 1024 * 1024

GRP2 = 4
GRP = 4
ROWS_P = 16
RC = 16
FCH = 512
FB = 2


def mm(a, b):
    return lax.dot_general(a, b, (((1,), (0,)), ((), ())), preferred_element_type=F32)


def mt(a, b):
    return lax.dot_general(a, b, (((1,), (1,)), ((), ())), preferred_element_type=F32)


def tm(a, b):
    return lax.dot_general(a, b, (((0,), (0,)), ((), ())), preferred_element_type=F32)


def norm(x):
    mean = jnp.mean(x, axis=-1, keepdims=True)
    centred = x - mean
    var = jnp.mean(centred * centred, axis=-1, keepdims=True)
    rstd = lax.rsqrt(var + EPS)
    return centred * rstd, rstd


def norm_back(n, xhat, rstd, gain):
    e = n * gain
    m1 = jnp.mean(e, axis=-1, keepdims=True)
    m2 = jnp.mean(e * xhat, axis=-1, keepdims=True)
    return rstd * (e - m1 - xhat * m2)


def fold8(a):
    return jnp.sum(a.reshape(a.shape[0] // 8, 8, a.shape[1]), axis=0)


def gelu_pair(h):
    e = jnp.exp2(h * h * (-0.5 * LOG2E))
    d = 1.0 + (0.3275911 * 2**-0.5) * jnp.abs(h)
    t = pl.reciprocal(d, approx=True)
    t = t * (2.0 - d * t)
    poly = 0.5 * 1.061405429
    for c in (-1.453152027, 1.421413741, -0.284496736, 0.254829592):
        poly = poly * t + 0.5 * c
    q = poly * t * e
    cdf = jnp.where(h >= 0, 1.0 - q, q)
    return h * cdf, cdf + h * e * (2 * np.pi) ** -0.5


def put_rows(ref, start, x):
    for c in range(HEADS):
        ref[c, start : start + x.shape[0]] = x[:, c * 128 : c * 128 + 128]


def get_row(ref, r, tot):
    return jnp.concatenate([ref[c, pl.ds(r, tot, stride=RC), :] for c in range(HEADS)], axis=1)


def full(shape):
    return pl.BlockSpec(shape, lambda *_: (0,) * len(shape), pipeline_mode=pl.Buffered(1))


def feature_forward_kernel(*refs, n, feats):
    x_refs, (gain, shift, wqkv, bias), outs = refs[:n], refs[n : n + 4], refs[n + 4 :]
    h_refs, (qkv_ref, p_ref), (xs, low, hs) = outs[:n], outs[n : n + 2], outs[n + 2 :]
    tot = n * feats
    pair = 2 * tot
    wide = bias.shape[1]
    for k in range(n):
        put_rows(xs, k * feats * RC, x_refs[k][...].reshape(feats * RC, D).astype(F32))
    for r in range(RC):
        xhat, _ = norm(get_row(xs, r, tot))
        low[r * tot : (r + 1) * tot] = (xhat * gain[...] + shift[...]).astype(BF)
    rows = tot * RC
    qkv_ref[0, :rows] = mm(low[...], wqkv[...]).astype(BF)
    qkv_ref[0, rows:] = jnp.zeros((qkv_ref.shape[1] - rows, QKV), BF)
    mask = bias[...]
    for b0 in range(0, RC // 2, GRP):
        jobs = [(b, h) for b in range(b0, b0 + GRP) for h in range(HEADS)]
        at = lambda b, h, c, w: (0, slice(b * pair, b * pair + w), slice(c * D + h * 128, c * D + h * 128 + 128))
        ss = [mt(qkv_ref[at(b, h, 0, pair)], qkv_ref[at(b, h, 1, wide)]) * (SCALE * LOG2E) + mask for b, h in jobs]
        es = [jnp.exp2(s - jnp.max(s, axis=-1, keepdims=True)) for s in ss]
        ps = [(e * (1.0 / jnp.sum(e, axis=-1, keepdims=True))).astype(BF) for e in es]
        os = [mm(p, qkv_ref[at(b, h, 2, wide)]) for p, (b, h) in zip(ps, jobs)]
        for p, o, (b, h) in zip(ps, os, jobs):
            p_ref[0, b, h] = p
            for j in range(2):
                hs[h, pl.ds(2 * b + j, tot, stride=RC), :] = o[j * tot : (j + 1) * tot]
    for k in range(n):
        for h in range(HEADS):
            h_refs[k][:, :, h * 128 : h * 128 + 128] = hs[h, k * feats * RC : (k + 1) * feats * RC].reshape(feats, RC, 128).astype(BF)


def feature_forward(xs, gain, shift, wqkv, bias):
    n = len(xs)
    feats, rows, _ = xs[0].shape
    tot = n * feats
    steps = rows // RC
    pad = tot * RC - 2 * tot + bias.shape[1]
    blk = pl.BlockSpec((feats, RC, D), lambda i: (0, i, 0))
    return pl.pallas_call(
        lambda *r: feature_forward_kernel(*r, n=n, feats=feats),
        grid=(steps,),
        in_specs=[blk] * n + [full((1, D)), full((1, D)), full((D, QKV)), full(bias.shape)],
        out_specs=[blk] * n
        + [
            pl.BlockSpec((1, pad, QKV), lambda i: (i, 0, 0)),
            pl.BlockSpec((1, RC // 2, HEADS, 2 * tot, bias.shape[1]), lambda i: (i, 0, 0, 0, 0)),
        ],
        out_shape=[jax.ShapeDtypeStruct((feats, rows, D), BF)] * n
        + [
            jax.ShapeDtypeStruct((steps, pad, QKV), BF),
            jax.ShapeDtypeStruct((steps, RC // 2, HEADS, 2 * tot, bias.shape[1]), BF),
        ],
        scratch_shapes=[
            pltpu.VMEM((HEADS, tot * RC, 128), F32),
            pltpu.VMEM((tot * RC, D), BF),
            pltpu.VMEM((HEADS, tot * RC, 128), F32),
        ],
        compiler_params=pltpu.CompilerParams(vmem_limit_bytes=VMEM),
        cost_estimate=pl.CostEstimate(flops=2 * tot * rows * D * QKV, bytes_accessed=24 * 10**6, transcendentals=0),
        name="feature_forward",
    )(*xs, gain, shift, wqkv, bias)


def feature_backward_kernel(*refs, n, feats):
    x_refs, g_refs, (qkv_ref, p_ref, gain, shift, wqkv), others, outs = refs[:n], refs[n : 2 * n], refs[2 * n : 2 * n + 5], refs[2 * n + 5 : 2 * n + 9], refs[2 * n + 9 :]
    d_refs, (dw_ref,), (dgain, dshift, vecs, xs, gs, ns, low, gh, gqkv, acc) = outs[:n], outs[n : n + 1], outs[n + 1 :]
    tot = n * feats
    pair = 2 * tot
    wide = p_ref.shape[-1]
    i = pl.program_id(0)

    @pl.when(i == 0)
    def _():
        acc[...] = jnp.zeros_like(acc)
        dgain[...] = jnp.zeros_like(dgain)
        dshift[...] = jnp.zeros_like(dshift)

    for k in range(n):
        put_rows(xs, k * feats * RC, x_refs[k][...].reshape(feats * RC, D).astype(F32))
        put_rows(gs, k * feats * RC, g_refs[k][...].reshape(feats * RC, D).astype(F32))
    for r in range(RC):
        gh[r * tot : (r + 1) * tot] = get_row(gs, r, tot).astype(BF)
        xhat, _ = norm(get_row(xs, r, tot))
        low[r * tot : (r + 1) * tot] = (xhat * gain[...] + shift[...]).astype(BF)
    for b0 in range(0, RC // 2, GRP):
        jobs = [(b, h) for b in range(b0, b0 + GRP) for h in range(HEADS)]
        at = lambda b, h, c, w: (0, slice(b * pair, b * pair + w), slice(c * D + h * 128, c * D + h * 128 + 128))
        gs_ = [gh[b * pair : (b + 1) * pair, h * 128 : h * 128 + 128] for b, h in jobs]
        dps = [mt(g, qkv_ref[at(b, h, 2, wide)]) for g, (b, h) in zip(gs_, jobs)]
        ps = [p_ref[0, b, h] for b, h in jobs]
        dvs = [tm(p, g) for p, g in zip(ps, gs_)]
        pds = [p.astype(F32) * dp for p, dp in zip(ps, dps)]
        dss = [(pd - p.astype(F32) * jnp.sum(pd, axis=-1, keepdims=True)).astype(BF) for p, pd in zip(ps, pds)]
        dqs = [mm(ds, qkv_ref[at(b, h, 1, wide)]) for ds, (b, h) in zip(dss, jobs)]
        dks = [tm(ds, qkv_ref[at(b, h, 0, pair)]) for ds, (b, h) in zip(dss, jobs)]
        for (b, h), dq, dk, dv in zip(jobs, dqs, dks, dvs):
            span = slice(b * pair, (b + 1) * pair)
            gqkv[span, h * 128 : h * 128 + 128] = (dq * SCALE).astype(BF)
            gqkv[span, D + h * 128 : D + h * 128 + 128] = (dk * SCALE).astype(BF)[:pair]
            gqkv[span, 2 * D + h * 128 : 2 * D + h * 128 + 128] = dv.astype(BF)[:pair]
    acc[...] += tm(low[...], gqkv[...])
    ns[...] = mt(gqkv[...], wqkv[...])
    for r in range(RC):
        xhat, rstd = norm(get_row(xs, r, tot))
        nn = ns[r * tot : (r + 1) * tot]
        dgain[...] += fold8(nn * xhat)
        dshift[...] += fold8(nn)
        d = norm_back(nn, xhat, rstd, gain[...])
        for c in range(HEADS):
            xs[c, pl.ds(r, tot, stride=RC), :] = d[:, c * 128 : c * 128 + 128]
    for k in range(n):
        for c in range(HEADS):
            d_refs[k][:, :, c * 128 : c * 128 + 128] = xs[c, k * feats * RC : (k + 1) * feats * RC].reshape(feats, RC, 128).astype(BF)

    @pl.when(i == pl.num_programs(0) - 1)
    def _():
        dw_ref[:, :QKV] = acc[...].astype(BF)
        vecs[...] = jnp.zeros_like(vecs)
        for j, v in enumerate((dgain, dshift) + others):
            vecs[j : j + 1] = jnp.sum(v[...], axis=0, keepdims=True)
        dw_ref[:, QKV:] = vecs[...].T.astype(BF)


def feature_backward(xs, gs, qkv, p, gain, shift, wqkv, others):
    n = len(xs)
    feats, rows, _ = xs[0].shape
    tot = n * feats
    steps = rows // RC
    blk = pl.BlockSpec((feats, RC, D), lambda i: (0, i, 0))
    return pl.pallas_call(
        lambda *r: feature_backward_kernel(*r, n=n, feats=feats),
        grid=(steps,),
        in_specs=[blk] * (2 * n)
        + [
            pl.BlockSpec((1,) + qkv.shape[1:], lambda i: (i, 0, 0)),
            pl.BlockSpec((1,) + p.shape[1:], lambda i: (i, 0, 0, 0, 0)),
            full((1, D)),
            full((1, D)),
            full((D, QKV)),
        ]
        + [full((8, D))] * 4,
        out_specs=[blk] * n + [pl.BlockSpec((D, QKV + 128), lambda i: (0, 0))],
        out_shape=[jax.ShapeDtypeStruct((feats, rows, D), BF)] * n + [jax.ShapeDtypeStruct((D, QKV + 128), BF)],
        scratch_shapes=[
            pltpu.VMEM((8, D), F32),
            pltpu.VMEM((8, D), F32),
            pltpu.VMEM((128, D), F32),
            pltpu.VMEM((HEADS, tot * RC, 128), F32),
            pltpu.VMEM((HEADS, tot * RC, 128), F32),
            pltpu.VMEM((tot * RC, D), F32),
            pltpu.VMEM((tot * RC, D), BF),
            pltpu.VMEM((tot * RC, D), BF),
            pltpu.VMEM((tot * RC, QKV), BF),
            pltpu.VMEM((D, QKV), F32),
        ],
        compiler_params=pltpu.CompilerParams(vmem_limit_bytes=VMEM),
        cost_estimate=pl.CostEstimate(flops=4 * tot * rows * D * QKV, bytes_accessed=30 * 10**6, transcendentals=0),
        name="feature_backward",
    )(*xs, *gs, qkv, p, gain, shift, wqkv, *others)


class Flat:
    def __init__(self, ref):
        self.ref = ref

    def __getitem__(self, key):
        rows, cols = (slice(None), slice(None)) if key is Ellipsis else key
        r = self.ref.shape[1]
        if rows.start is not None:
            rows = slice(rows.start // r, rows.stop // r)
        w = self.ref[rows, :, cols]
        return w.reshape(w.shape[0] * w.shape[1], w.shape[2])


def unpack_copies(pack, weights, sems):
    copies, at = [], 0
    for w in weights:
        r = w.shape[1]
        for j in range(w.shape[2] // D):
            src = pack.at[:, pl.ds(at, r), :]
            copies.append(pltpu.make_async_copy(src, w.at[:, :, pl.ds(j * D, D)], sems.at[len(copies)]))
            at += r
    return copies


def middle_kernel(me_ref, *refs, n, rows, part):
    it = iter(refs)
    take = lambda c: [next(it) for _ in range(c)]
    (x_ref,) = take(1)
    h_refs = take(n)
    cot_ref, bias, pack, g2, b2, g3, b3 = take(7)
    out_ref, gaf_ref = take(2)
    gh_refs = take(n)
    dpack, dg2, db2, dg3, db3 = take(5)
    h1_s, qkv_s, p_s, gq_s, heads_s, gh2_s, afo, arq, aro, ain, aout, wfo_s, wrq_s, wro_s, win_s, wout_s, sems = take(17)
    i = pl.program_id(0)
    me = me_ref[0]
    m = FB * rows

    @pl.when(i == 0)
    def _():
        copies = unpack_copies(pack, (wfo_s, wrq_s, wro_s, win_s, wout_s), sems)
        for c in copies:
            c.start()
        for a in (afo, arq, aro, ain, aout, dg2, db2, dg3, db3):
            a[...] = jnp.zeros_like(a)
        for c in copies:
            c.wait()

    wfo, wrq, wro, win, wout = (Flat(w) for w in (wfo_s, wrq_s, wro_s, win_s, wout_s))
    for k in range(n):
        off = pl.multiple_of((me ^ k) * part, part)
        for f in range(FB):
            h1_s[pl.ds(f * rows + off, part), :] = h_refs[k][f]
    x = x_ref[0].reshape(m, D).astype(F32)
    h1 = h1_s[...]
    after_feat = x + mm(h1, wfo[...])
    xhat2, rstd2 = norm(after_feat)
    low2 = (xhat2 * g2[...] + b2[...]).astype(BF)
    qkv_s[...] = mm(low2, wrq[...]).astype(BF)
    mask = bias[...]
    jobs = [(f, h) for f in range(FB) for h in range(HEADS)]
    at = lambda f, h, c: (slice(f * rows, (f + 1) * rows), slice(c * D + h * 128, c * D + h * 128 + 128))
    for g0 in range(0, len(jobs), GRP2):
        some = jobs[g0 : g0 + GRP2]
        ss = [mt(qkv_s[at(f, h, 0)], qkv_s[at(f, h, 1)]) * (SCALE * LOG2E) + mask for f, h in some]
        es = [jnp.exp2(s - jnp.max(s, axis=-1, keepdims=True)) for s in ss]
        ps = [(e * (1.0 / jnp.sum(e, axis=-1, keepdims=True))).astype(BF) for e in es]
        for p, (f, h) in zip(ps, some):
            p_s[f * HEADS + h] = p
            heads_s[at(f, h, 0)] = mm(p, qkv_s[at(f, h, 2)]).astype(BF)
    heads = heads_s[...]
    after_row = after_feat + mm(heads, wro[...])
    xhat3, rstd3 = norm(after_row)
    low3 = (xhat3 * g3[...] + b3[...]).astype(BF)
    cot = cot_ref[0].reshape(m, D)
    out = after_row
    n3 = None
    for j in range(FF // FCH):
        cols = slice(j * FCH, (j + 1) * FCH)
        act, slope = gelu_pair(mm(low3, win[:, cols]))
        act = act.astype(BF)
        out = out + mm(act, wout[cols, :])
        ghid = (mt(cot, wout[cols, :]) * slope).astype(BF)
        aout[:, cols] += tm(cot, act)
        ain[:, cols] += tm(low3, ghid)
        back = mt(ghid, win[:, cols])
        n3 = back if n3 is None else n3 + back
    out_ref[0] = out.astype(BF).reshape(FB, rows, D)
    dg3[...] += fold8(n3 * xhat3)
    db3[...] += fold8(n3)
    g_row = cot.astype(F32) + norm_back(n3, xhat3, rstd3, g3[...])
    gb = g_row.astype(BF)
    aro[...] += tm(heads, gb)
    gh2_s[...] = mt(gb, wro[...]).astype(BF)
    for g0 in range(0, len(jobs), GRP2):
        some = jobs[g0 : g0 + GRP2]
        gs = [gh2_s[at(f, h, 0)] for f, h in some]
        ps = [p_s[f * HEADS + h] for f, h in some]
        dps = [mt(g, qkv_s[at(f, h, 2)]) for g, (f, h) in zip(gs, some)]
        pds = [p.astype(F32) * dp for p, dp in zip(ps, dps)]
        dss = [(pd - p.astype(F32) * jnp.sum(pd, axis=-1, keepdims=True)).astype(BF) for p, pd in zip(ps, pds)]
        for (f, h), g, p, ds in zip(some, gs, ps, dss):
            gq_s[at(f, h, 2)] = tm(p, g).astype(BF)
            gq_s[at(f, h, 0)] = (mm(ds, qkv_s[at(f, h, 1)]) * SCALE).astype(BF)
            gq_s[at(f, h, 1)] = (tm(ds, qkv_s[at(f, h, 0)]) * SCALE).astype(BF)
    gq = gq_s[...]
    arq[...] += tm(low2, gq)
    n2 = mt(gq, wrq[...])
    dg2[...] += fold8(n2 * xhat2)
    db2[...] += fold8(n2)
    g_feat = g_row + norm_back(n2, xhat2, rstd2, g2[...])
    gaf_ref[...] = g_feat.reshape(FB, rows, D)
    gf = g_feat.astype(BF)
    afo[...] += tm(h1, gf)
    h1_s[...] = mt(gf, wfo[...]).astype(BF)
    for k in range(n):
        off = pl.multiple_of((me ^ k) * part, part)
        for f in range(FB):
            gh_refs[k][f] = h1_s[pl.ds(f * rows + off, part), :]

    @pl.when(i == pl.num_programs(0) - 1)
    def _():
        at = 0
        for acc in (afo, arq, aro, ain):
            for j in range(acc.shape[1] // D):
                dpack[:, at : at + ROWS_P, :] = acc[:, j * D : (j + 1) * D].astype(BF).reshape(D // ROWS_P, ROWS_P, D)
                at += ROWS_P
        for j in range(FF // D):
            dpack[j * 8 : (j + 1) * 8, at:, :] = aout[:, j * D : (j + 1) * D].T.astype(BF).reshape(8, 4 * ROWS_P, D)


def middle(me, x, hs, cot, bias, pack, g2, b2, g3, b3):
    n = len(hs)
    _, feats, rows, _ = x.shape
    part = rows // n
    m = FB * rows
    xblk = pl.BlockSpec((1, FB, rows, D), lambda i, me: (0, i, 0, 0))
    hblk = pl.BlockSpec((FB, part, D), lambda i, me: (i, 0, 0))
    acc = lambda *s: pl.BlockSpec(s, lambda i, me: (0, 0))
    sds = jax.ShapeDtypeStruct
    return pl.pallas_call(
        lambda *r: middle_kernel(*r, n=n, rows=rows, part=part),
        grid_spec=pltpu.PrefetchScalarGridSpec(
            num_scalar_prefetch=1,
            grid=(feats // FB,),
            in_specs=[xblk]
            + [hblk] * n
            + [
                xblk,
                full((rows, rows)),
                pl.BlockSpec(memory_space=pl.ANY),
                full((1, D)),
                full((1, D)),
                full((1, D)),
                full((1, D)),
            ],
            out_specs=[xblk, pl.BlockSpec((FB, rows, D), lambda i, me: (i, 0, 0))]
            + [hblk] * n
            + [pl.BlockSpec(pack.shape, lambda i, me: (0, 0, 0))]
            + [acc(8, D)] * 4,
            scratch_shapes=[
                pltpu.VMEM((m, D), BF),
                pltpu.VMEM((m, QKV), BF),
                pltpu.VMEM((FB * HEADS, rows, rows), BF),
                pltpu.VMEM((m, QKV), BF),
                pltpu.VMEM((m, D), BF),
                pltpu.VMEM((m, D), BF),
                pltpu.VMEM((D, D), F32),
                pltpu.VMEM((D, QKV), F32),
                pltpu.VMEM((D, D), F32),
                pltpu.VMEM((D, FF), F32),
                pltpu.VMEM((D, FF), F32),
                pltpu.VMEM((32, ROWS_P, D), BF),
                pltpu.VMEM((32, ROWS_P, QKV), BF),
                pltpu.VMEM((32, ROWS_P, D), BF),
                pltpu.VMEM((32, ROWS_P, FF), BF),
                pltpu.VMEM((32, 4 * ROWS_P, D), BF),
                pltpu.SemaphoreType.DMA((10,)),
            ],
        ),
        out_shape=[sds(x.shape, BF), sds((feats, rows, D), F32)]
        + [sds((feats, part, D), BF)] * n
        + [sds(pack.shape, BF)]
        + [sds((8, D), F32)] * 4,
        compiler_params=pltpu.CompilerParams(vmem_limit_bytes=VMEM),
        cost_estimate=pl.CostEstimate(flops=70 * 10**9, bytes_accessed=50 * 10**6, transcendentals=0),
        name="middle",
    )(me, x, *hs, cot, bias, pack, g2, b2, g3, b3)


def final_kernel(me_ref, g_ref, *refs, n, part):
    d_refs, out = refs[:n], refs[n]
    me = me_ref[0]
    for k in range(n):
        off = pl.multiple_of((me ^ k) * part, part)
        out[0, :, pl.ds(off, part), :] = g_ref[:, pl.ds(off, part), :] + d_refs[k][...].astype(F32)


def final(me, g, ds):
    n = len(ds)
    feats, rows, _ = g.shape
    part = rows // n
    fb = 3
    return pl.pallas_call(
        lambda *r: final_kernel(*r, n=n, part=part),
        grid_spec=pltpu.PrefetchScalarGridSpec(
            num_scalar_prefetch=1,
            grid=(feats // fb,),
            in_specs=[pl.BlockSpec((fb, rows, D), lambda i, me: (i, 0, 0))] + [pl.BlockSpec((fb, part, D), lambda i, me: (i, 0, 0))] * n,
            out_specs=pl.BlockSpec((1, fb, rows, D), lambda i, me: (0, i, 0, 0)),
        ),
        out_shape=jax.ShapeDtypeStruct((1, feats, rows, D), F32),
        compiler_params=pltpu.CompilerParams(vmem_limit_bytes=VMEM),
        name="final",
    )(me, g, *ds)


def row_allowed(segments, context):
    tables = jnp.arange(context.shape[0], dtype=jnp.int32)
    member = (segments[:, None] == tables[None, :]).astype(jnp.int32)
    sizes = jnp.sum(member, axis=0)
    starts = jnp.cumsum(sizes) - sizes
    places = jnp.arange(segments.shape[0], dtype=jnp.int32) - jnp.sum(member * starts[None, :], axis=1)
    limits = jnp.sum(member * context[None, :], axis=1)
    usable = places < limits
    return (segments[:, None] == segments[None, :]) & usable[None, :]


def swap(arrays, n):
    return [arrays[0]] + [lax.ppermute(arrays[k], "feat", [(d, d ^ k) for d in range(n)]) for k in range(1, n)]


class Shards:
    def __init__(self, rows, n):
        self.count = rows * n
        self.bits = [("rows", 1 << b) for b in reversed(range(rows.bit_length() - 1))]
        self.bits += [("feat", 1 << b) for b in reversed(range(n.bit_length() - 1))]
        self.sizes = {"rows": rows, "feat": n}
        last = len(self.bits) - 1
        self.rows_bits = list(range(rows.bit_length() - 1))
        self.near = last
        self.feat_bits = list(range(rows.bit_length() - 1, last))

    def other(self, a, at):
        axis, bit = self.bits[at]
        return lax.ppermute(a, axis, [(d, d ^ bit) for d in range(self.sizes[axis])])

    def side(self, at):
        axis, bit = self.bits[at]
        return (lax.axis_index(axis) // bit) % 2

    def gather(self, a, order):
        shape = a.shape
        a = a.reshape((1,) * len(self.bits) + shape)
        for at in order:
            b = self.other(a, at)
            low = self.side(at) == 0
            a = jnp.concatenate([jnp.where(low, a, b), jnp.where(low, b, a)], axis=at)
        return a.reshape((self.count,) + shape)

    def scatter(self, a, order):
        shape = a.shape[1:]
        a = a.reshape((2,) * len(self.bits) + shape)
        for step, at in enumerate(order):
            side = self.side(at)
            sent = self.other(lax.dynamic_index_in_dim(a, 1 - side, at, True), at)
            a = lax.dynamic_index_in_dim(a, side, at, True).astype(F32) + sent.astype(F32)
            if step < len(order) - 1:
                a = a.astype(BF)
        return a.reshape(shape)


def pack_shards(mats, down):
    return jnp.concatenate([m[:, j * D : (j + 1) * D] for m in mats for j in range(m.shape[1] // D)] + [down], axis=0)


def repack(a, blocks):
    count = a.shape[0]
    if count == blocks:
        return a
    r, q = D // count, D // blocks
    parts = [a[:, j * r : (j + 1) * r].reshape(blocks, q, D) for j in range(9)]
    return jnp.concatenate(parts + [a[:, 9 * r :].reshape(blocks, 4 * q, D)], axis=1)


def per_device(rows_axis, n, inputs, *rest):
    weights, (cotangent, segments, context, feature_mask) = rest[:12], rest[12:]
    gain_one, shift_one, qkv_one, out_one, gain_two, shift_two, qkv_two, out_two, gain_three, shift_three, up, down = weights
    shards = Shards(rows_axis, n)
    _, feats, rows, _ = inputs.shape
    part = rows // n
    tot = n * feats
    me = lax.axis_index("feat").astype(jnp.int32)
    me_arr = me.reshape(1)

    vectors = jnp.stack((gain_one, shift_one, gain_two, shift_two, gain_three, shift_three), axis=1)
    first = jnp.concatenate([qkv_one, jnp.pad(vectors, ((0, 0), (0, 128 - 6)))], axis=1)
    first = shards.gather(first, shards.feat_bits + shards.rows_bits + [shards.near]).reshape(D, QKV + 128)
    pack = lax.all_gather(pack_shards((out_one, qkv_two, out_two, up), down), ("rows", "feat"), axis=0)
    pack = repack(pack, D // ROWS_P)
    gains = first[:, QKV : QKV + 6].astype(F32).T
    g1, b1, g2, b2, g3, b3 = [gains[j : j + 1] for j in range(6)]

    mine = [lax.dynamic_slice(inputs[0], (0, (me ^ k) * part, 0), (feats, part, D)) for k in range(n)]
    xs = swap(mine, n)
    order = me ^ jnp.arange(n, dtype=jnp.int32)
    valid = jnp.take(feature_mask[0].reshape(n, feats), order, axis=0).reshape(tot) > 0
    wide = -(-2 * tot // 128) * 128
    lane = jnp.arange(wide)
    same = (lane[None, :] // tot == jnp.arange(2 * tot)[:, None] // tot) & (lane < 2 * tot)[None, :]
    bias_one = jnp.where(same & jnp.pad(jnp.tile(valid, 2), (0, wide - 2 * tot))[None, :], 0.0, MASKED).astype(F32)
    bias_two = jnp.where(row_allowed(segments[0], context[0]), 0.0, MASKED).astype(F32)

    *heads, qkv, p = feature_forward(xs, g1, b1, first, bias_one)
    hs = swap(heads, n)
    res = middle(me_arr, inputs, hs, cotangent, bias_two, pack, g2, b2, g3, b3)
    output, gaf, gh = res[0], res[1], res[2 : 2 + n]
    dpack, dg2, db2, dg3, db3 = res[2 + n :]
    gs = swap(gh, n)
    *dx, dfirst = feature_backward(xs, gs, qkv, p, g1, b1, first, (dg2, db2, dg3, db3))
    back = swap(dx, n)
    input_grad = final(me_arr, gaf, back)

    down_order = [shards.near] + shards.rows_bits[::-1] + shards.feat_bits
    dpack = shards.scatter(repack(dpack, shards.count), down_order)
    dfirst = shards.scatter(dfirst.reshape(shards.count, -1, QKV + 128), down_order)
    r = D // shards.count
    cut = lambda a, b: jnp.concatenate([dpack[j * r : (j + 1) * r] for j in range(a, b)], axis=1)
    v = [dfirst[:, QKV + j] for j in range(6)]
    return (output, input_grad, v[0], v[1], dfirst[:, :QKV], cut(0, 1), v[2], v[3], cut(1, 4), cut(4, 5), v[4], v[5], cut(5, 9), dpack[9 * r :])


def solution(mesh):
    rows_axis, n = mesh.shape["rows"], mesh.shape["feat"]
    vec, mat, act, tab = P(("rows", "feat")), P(("rows", "feat"), None), P("rows", "feat", None, None), P("rows", None)
    weights = (vec, vec, mat, mat, vec, vec, mat, mat, vec, vec, mat, mat)
    return jax.shard_map(
        lambda *a: per_device(rows_axis, n, *a),
        mesh=mesh,
        in_specs=(act,) + weights + (act, tab, tab, tab),
        out_specs=(act, act) + weights,
        check_vma=False,
    )
```

```python
import jax
import jax.numpy as jnp
import numpy as np
from jax import lax
from jax.experimental import pallas as pl
from jax.experimental.pallas import tpu as pltpu
from jax.sharding import PartitionSpec as P

D = 512
HEADS = 4
HEAD_DIM = 128
FF = 2048
QKV = 3 * D
EPS = 1e-05
MASKED = -1e30
SCALE = HEAD_DIM**-0.5
BF = jnp.bfloat16
F32 = jnp.float32
LOG2E = float(np.log2(np.e))
VMEM = 60 * 1024 * 1024

GRP2 = 4
GRP = 4
ROWS_P = 16
COST = pl.CostEstimate(flops=10**11, bytes_accessed=10**6, transcendentals=0)
RC = 16
FCH = 512
FB = 2


def mm(a, b):
    return lax.dot_general(a, b, (((1,), (0,)), ((), ())), preferred_element_type=F32)


def mt(a, b):
    return lax.dot_general(a, b, (((1,), (1,)), ((), ())), preferred_element_type=F32)


def tm(a, b):
    return lax.dot_general(a, b, (((0,), (0,)), ((), ())), preferred_element_type=F32)


def norm(x):
    mean = jnp.mean(x, axis=-1, keepdims=True)
    centred = x - mean
    var = jnp.mean(centred * centred, axis=-1, keepdims=True)
    rstd = lax.rsqrt(var + EPS)
    return centred * rstd, rstd


def norm_back(n, xhat, rstd, gain):
    e = n * gain
    m1 = jnp.mean(e, axis=-1, keepdims=True)
    m2 = jnp.mean(e * xhat, axis=-1, keepdims=True)
    return rstd * (e - m1 - xhat * m2)


def fold8(a):
    return jnp.sum(a.reshape(a.shape[0] // 8, 8, a.shape[1]), axis=0)


def gelu_pair(h):
    e = jnp.exp2(h * h * (-0.5 * LOG2E))
    d = 1.0 + (0.3275911 * 2**-0.5) * jnp.abs(h)
    t = pl.reciprocal(d, approx=True)
    t = t * (2.0 - d * t)
    poly = 0.5 * 1.061405429
    for c in (-1.453152027, 1.421413741, -0.284496736, 0.254829592):
        poly = poly * t + 0.5 * c
    q = poly * t * e
    cdf = jnp.where(h >= 0, 1.0 - q, q)
    return h * cdf, cdf + h * e * (2 * np.pi) ** -0.5


def put_rows(ref, start, x):
    for c in range(HEADS):
        ref[c, start : start + x.shape[0]] = x[:, c * 128 : c * 128 + 128]


def get_row(ref, r, tot):
    return jnp.concatenate([ref[c, pl.ds(r, tot, stride=RC), :] for c in range(HEADS)], axis=1)


def full(shape):
    return pl.BlockSpec(shape, lambda *_: (0,) * len(shape), pipeline_mode=pl.Buffered(1))


def feature_forward_kernel(_, *refs, n, feats, cuts):
    x_refs, (gain, shift, wqkv, bias), outs = refs[:n], refs[n : n + 4], refs[n + 4 :]
    nc = n * len(cuts)
    h_refs, (qkv_ref, p_ref), (xs, low, hs) = outs[:nc], outs[nc : nc + 2], outs[nc + 2 :]
    tot = n * feats
    pair = 2 * tot
    wide = bias.shape[1]
    for k in range(n):
        put_rows(xs, k * feats * RC, x_refs[k][...].reshape(feats * RC, D).astype(F32))
    for r in range(RC):
        xhat, _ = norm(get_row(xs, r, tot))
        low[r * tot : (r + 1) * tot] = (xhat * gain[...] + shift[...]).astype(BF)
    rows = tot * RC
    qkv_ref[0, :rows] = mm(low[...], wqkv[...]).astype(BF)
    qkv_ref[0, rows:] = jnp.zeros((qkv_ref.shape[1] - rows, QKV), BF)
    mask = bias[...]
    for b0 in range(0, RC // 2, GRP):
        jobs = [(b, h) for b in range(b0, b0 + GRP) for h in range(HEADS)]
        at = lambda b, h, c, w: (0, slice(b * pair, b * pair + w), slice(c * D + h * 128, c * D + h * 128 + 128))
        ss = [mt(qkv_ref[at(b, h, 0, pair)], qkv_ref[at(b, h, 1, wide)]) * (SCALE * LOG2E) + mask for b, h in jobs]
        es = [jnp.exp2(s - jnp.max(s, axis=-1, keepdims=True)) for s in ss]
        ps = [(e * (1.0 / jnp.sum(e, axis=-1, keepdims=True))).astype(BF) for e in es]
        os = [mm(p, qkv_ref[at(b, h, 2, wide)]) for p, (b, h) in zip(ps, jobs)]
        for p, o, (b, h) in zip(ps, os, jobs):
            p_ref[0, b, h] = p
            for j in range(2):
                hs[h, pl.ds(2 * b + j, tot, stride=RC), :] = o[j * tot : (j + 1) * tot]
    for c, (f0, f1) in enumerate(cuts):
        for k in range(n):
            for h in range(HEADS):
                part = hs[h, (k * feats + f0) * RC : (k * feats + f1) * RC].reshape(f1 - f0, RC, 128)
                h_refs[c * n + k][:, :, h * 128 : h * 128 + 128] = part.astype(BF)


def feature_forward(x_rows, xs, gain, shift, wqkv, bias, cuts, rows):
    n = len(xs)
    feats = xs[0].shape[0]
    tot = n * feats
    steps = rows // RC
    pad = tot * RC - 2 * tot + bias.shape[1]
    sds = jax.ShapeDtypeStruct
    return pl.pallas_call(
        lambda *r: feature_forward_kernel(*r, n=n, feats=feats, cuts=cuts),
        grid_spec=pltpu.PrefetchScalarGridSpec(
            num_scalar_prefetch=1,
            grid=(steps,),
            in_specs=[pl.BlockSpec((feats, RC, D), lambda i, at, k=k: (0, i + at[k], 0)) for k in range(n)]
            + [full((1, D)), full((1, D)), full((D, QKV)), full(bias.shape)],
            out_specs=[pl.BlockSpec((f1 - f0, RC, D), lambda i, at: (0, i, 0)) for f0, f1 in cuts for _ in range(n)]
            + [
                pl.BlockSpec((1, pad, QKV), lambda i, at: (i, 0, 0)),
                pl.BlockSpec((1, RC // 2, HEADS, 2 * tot, bias.shape[1]), lambda i, at: (i, 0, 0, 0, 0)),
            ],
            scratch_shapes=[
                pltpu.VMEM((HEADS, tot * RC, 128), F32),
                pltpu.VMEM((tot * RC, D), BF),
                pltpu.VMEM((HEADS, tot * RC, 128), F32),
            ],
        ),
        out_shape=[sds((f1 - f0, rows, D), BF) for f0, f1 in cuts for _ in range(n)]
        + [sds((steps, pad, QKV), BF), sds((steps, RC // 2, HEADS, 2 * tot, bias.shape[1]), BF)],
        compiler_params=pltpu.CompilerParams(vmem_limit_bytes=VMEM),
        cost_estimate=COST,
        name="feature_forward",
    )(x_rows, *xs, gain, shift, wqkv, bias)


def feature_backward_kernel(_, *refs, n, feats, cuts, first, last):
    it = iter(refs)
    take = lambda c: [next(it) for _ in range(c)]
    x_refs = take(n)
    g_refs = take(n * len(cuts))
    qkv_ref, p_ref, gain, shift, wqkv = take(5)
    carried = [] if first else take(3)
    others = take(4) if last else []
    d_refs = take(n)
    outs = take(1) if last else take(3)
    dgain, dshift, vecs, xs, gs, ns, low, gh, gqkv, acc = take(10)
    if not last:
        acc, dgain, dshift = outs
    tot = n * feats
    pair = 2 * tot
    wide = p_ref.shape[-1]
    i = pl.program_id(0)

    @pl.when(i == 0)
    def _():
        for j, a in enumerate((acc, dgain, dshift)):
            a[...] = jnp.zeros_like(a) if first else carried[j][...]

    for k in range(n):
        put_rows(xs, k * feats * RC, x_refs[k][...].reshape(feats * RC, D).astype(F32))
        for c, (f0, f1) in enumerate(cuts):
            put_rows(gs, (k * feats + f0) * RC, g_refs[c * n + k][...].reshape((f1 - f0) * RC, D).astype(F32))
    for r in range(RC):
        gh[r * tot : (r + 1) * tot] = get_row(gs, r, tot).astype(BF)
        xhat, _ = norm(get_row(xs, r, tot))
        low[r * tot : (r + 1) * tot] = (xhat * gain[...] + shift[...]).astype(BF)
    for b0 in range(0, RC // 2, GRP):
        jobs = [(b, h) for b in range(b0, b0 + GRP) for h in range(HEADS)]
        at = lambda b, h, c, w: (0, slice(b * pair, b * pair + w), slice(c * D + h * 128, c * D + h * 128 + 128))
        gs_ = [gh[b * pair : (b + 1) * pair, h * 128 : h * 128 + 128] for b, h in jobs]
        dps = [mt(g, qkv_ref[at(b, h, 2, wide)]) for g, (b, h) in zip(gs_, jobs)]
        ps = [p_ref[0, b, h] for b, h in jobs]
        dvs = [tm(p, g) for p, g in zip(ps, gs_)]
        pds = [p.astype(F32) * dp for p, dp in zip(ps, dps)]
        dss = [(pd - p.astype(F32) * jnp.sum(pd, axis=-1, keepdims=True)).astype(BF) for p, pd in zip(ps, pds)]
        dqs = [mm(ds, qkv_ref[at(b, h, 1, wide)]) for ds, (b, h) in zip(dss, jobs)]
        dks = [tm(ds, qkv_ref[at(b, h, 0, pair)]) for ds, (b, h) in zip(dss, jobs)]
        for (b, h), dq, dk, dv in zip(jobs, dqs, dks, dvs):
            span = slice(b * pair, (b + 1) * pair)
            gqkv[span, h * 128 : h * 128 + 128] = (dq * SCALE).astype(BF)
            gqkv[span, D + h * 128 : D + h * 128 + 128] = (dk * SCALE).astype(BF)[:pair]
            gqkv[span, 2 * D + h * 128 : 2 * D + h * 128 + 128] = dv.astype(BF)[:pair]
    acc[...] += tm(low[...], gqkv[...])
    ns[...] = mt(gqkv[...], wqkv[...])
    for r in range(RC):
        xhat, rstd = norm(get_row(xs, r, tot))
        nn = ns[r * tot : (r + 1) * tot]
        dgain[...] += fold8(nn * xhat)
        dshift[...] += fold8(nn)
        d = norm_back(nn, xhat, rstd, gain[...])
        for c in range(HEADS):
            xs[c, pl.ds(r, tot, stride=RC), :] = d[:, c * 128 : c * 128 + 128]
    for k in range(n):
        for c in range(HEADS):
            d_refs[k][:, :, c * 128 : c * 128 + 128] = xs[c, k * feats * RC : (k + 1) * feats * RC].reshape(feats, RC, 128).astype(BF)

    if last:

        @pl.when(i == pl.num_programs(0) - 1)
        def _():
            outs[0][:, :QKV] = acc[...].astype(BF)
            vecs[...] = jnp.zeros_like(vecs)
            for j, v in enumerate([dgain, dshift] + others):
                vecs[j : j + 1] = jnp.sum(v[...], axis=0, keepdims=True)
            outs[0][:, QKV:] = vecs[...].T.astype(BF)


def feature_backward(x_rows, xs, gs, qkv, p, gain, shift, wqkv, cuts, r0, r1, carried, others):
    n = len(xs)
    feats = xs[0].shape[0]
    tot = n * feats
    s0, steps = r0 // RC, (r1 - r0) // RC
    first, last = not carried, bool(others)
    sds = jax.ShapeDtypeStruct
    at = lambda f, row: pl.BlockSpec((f, RC, D), lambda i, _: (0, i + (r0 - row) // RC, 0))
    sums = [(D, QKV), (8, D), (8, D)]
    if last:
        out_specs, out_shape = [pl.BlockSpec((D, QKV + 128), lambda i, _: (0, 0))], [sds((D, QKV + 128), BF)]
    else:
        out_specs, out_shape = [pl.BlockSpec(q, lambda i, _: (0, 0)) for q in sums], [sds(q, F32) for q in sums]
    return pl.pallas_call(
        lambda *r: feature_backward_kernel(*r, n=n, feats=feats, cuts=cuts, first=first, last=last),
        grid_spec=pltpu.PrefetchScalarGridSpec(
            num_scalar_prefetch=1,
            grid=(steps,),
            in_specs=[pl.BlockSpec((feats, RC, D), lambda i, q, k=k: (0, i + s0 + q[k], 0)) for k in range(n)]
            + [at(f1 - f0, row) for (f0, f1), (row, _) in zip(cuts, gs) for _ in range(n)]
            + [
                pl.BlockSpec((1,) + qkv.shape[1:], lambda i, _: (i + s0, 0, 0)),
                pl.BlockSpec((1,) + p.shape[1:], lambda i, _: (i + s0, 0, 0, 0, 0)),
                full((1, D)),
                full((1, D)),
                full((D, QKV)),
            ]
            + [full(q.shape) for q in carried]
            + [full((8, D)) for _ in others],
            out_specs=[at(feats, r0)] * n + out_specs,
            scratch_shapes=[
                pltpu.VMEM((8, D), F32),
                pltpu.VMEM((8, D), F32),
                pltpu.VMEM((128, D), F32),
                pltpu.VMEM((HEADS, tot * RC, 128), F32),
                pltpu.VMEM((HEADS, tot * RC, 128), F32),
                pltpu.VMEM((tot * RC, D), F32),
                pltpu.VMEM((tot * RC, D), BF),
                pltpu.VMEM((tot * RC, D), BF),
                pltpu.VMEM((tot * RC, QKV), BF),
                pltpu.VMEM((D, QKV), F32),
            ],
        ),
        out_shape=[sds((feats, r1 - r0, D), BF)] * n + out_shape,
        compiler_params=pltpu.CompilerParams(vmem_limit_bytes=VMEM),
        cost_estimate=COST,
        name="feature_backward",
    )(x_rows, *xs, *[a for _, part in gs for a in part], qkv, p, gain, shift, wqkv, *carried, *others)


class Flat:
    def __init__(self, ref):
        self.ref = ref

    def __getitem__(self, key):
        rows, cols = (slice(None), slice(None)) if key is Ellipsis else key
        r = self.ref.shape[1]
        if rows.start is not None:
            rows = slice(rows.start // r, rows.stop // r)
        w = self.ref[rows, :, cols]
        return w.reshape(w.shape[0] * w.shape[1], w.shape[2])


def unpack_copies(pack, weights, sems):
    copies, at = [], 0
    for w in weights:
        r = w.shape[1]
        for j in range(w.shape[2] // D):
            src = pack.at[:, pl.ds(at, r), :]
            copies.append(pltpu.make_async_copy(src, w.at[:, :, pl.ds(j * D, D)], sems.at[len(copies)]))
            at += r
    return copies


def middle_kernel(me_ref, core_ref, *refs, n, rows, part, spans, first, last):
    it = iter(refs)
    take = lambda c: [next(it) for _ in range(c)]
    (x_ref,) = take(1)
    h_refs = take(n)
    cot_ref, bias, pack, g2, b2, g3, b3 = take(7)
    carried = [] if first else take(9)
    _ = [] if first else take(2)
    out_ref, gaf_ref = take(2)
    gh_refs = take(n * len(spans))
    kept = take(2) if last else take(5)
    dg2, db2, dg3, db3 = take(4)
    h1_s, qkv_s, p_s, gq_s, heads_s, gh2_s, afo, arq, aro, ain, aout, wfo_s, wrq_s, wro_s, win_s, wout_s, sems, asems = take(18)
    i = pl.program_id(0)
    me = me_ref[0]
    m = FB * rows
    accs = (afo, arq, aro, ain, aout)

    @pl.when(i == 0)
    def _():
        copies = unpack_copies(pack, (wfo_s, wrq_s, wro_s, win_s, wout_s), sems)
        for c in copies:
            c.start()
        if first:
            for a in (afo, arq, aro, ain, aout, dg2, db2, dg3, db3):
                a[...] = jnp.zeros_like(a)
        else:
            more = [pltpu.make_async_copy(c, a, asems.at[j]) for j, (c, a) in enumerate(zip(carried, accs))]
            for c in more:
                c.start()
            for c, a in zip(carried[5:], (dg2, db2, dg3, db3)):
                a[...] = c[...]

    def need(*which):
        @pl.when(i == 0)
        def _():
            at = 0
            for j, w in enumerate((wfo_s, wrq_s, wro_s, win_s, wout_s)):
                for _ in range(w.shape[2] // D):
                    if j in which:
                        pltpu.make_async_copy(pack.at[:, pl.ds(0, w.shape[1]), :], w.at[:, :, pl.ds(0, D)], sems.at[at]).wait()
                    at += 1

    def settle(*which):
        if not first:

            @pl.when(i == 0)
            def _():
                for j in which:
                    pltpu.make_async_copy(carried[j], accs[j], asems.at[j]).wait()

    def keep(*which):
        if not last:

            @pl.when(i == pl.num_programs(0) - 1)
            def _():
                for j in which:
                    pltpu.make_async_copy(accs[j], kept[j], asems.at[j]).start()

    wfo, wrq, wro, win, wout = (Flat(w) for w in (wfo_s, wrq_s, wro_s, win_s, wout_s))
    for k in range(n):
        off = pl.multiple_of((me ^ k) * part, part)
        for f in range(FB):
            h1_s[pl.ds(f * rows + off, part), :] = h_refs[k][f]
    x = x_ref[0].reshape(m, D).astype(F32)
    h1 = h1_s[...]
    need(0)
    after_feat = x + mm(h1, wfo[...])
    xhat2, rstd2 = norm(after_feat)
    low2 = (xhat2 * g2[...] + b2[...]).astype(BF)
    need(1, 2, 3, 4)
    settle(3, 4)
    qkv_s[...] = mm(low2, wrq[...]).astype(BF)
    mask = bias[...]
    jobs = [(f, h) for f in range(FB) for h in range(HEADS)]
    at = lambda f, h, c: (slice(f * rows, (f + 1) * rows), slice(c * D + h * 128, c * D + h * 128 + 128))
    for g0 in range(0, len(jobs), GRP2):
        some = jobs[g0 : g0 + GRP2]
        ss = [mt(qkv_s[at(f, h, 0)], qkv_s[at(f, h, 1)]) * (SCALE * LOG2E) + mask for f, h in some]
        es = [jnp.exp2(s - jnp.max(s, axis=-1, keepdims=True)) for s in ss]
        ps = [(e * (1.0 / jnp.sum(e, axis=-1, keepdims=True))).astype(BF) for e in es]
        for p, (f, h) in zip(ps, some):
            p_s[f * HEADS + h] = p
            heads_s[at(f, h, 0)] = mm(p, qkv_s[at(f, h, 2)]).astype(BF)
    heads = heads_s[...]
    after_row = after_feat + mm(heads, wro[...])
    xhat3, rstd3 = norm(after_row)
    low3 = (xhat3 * g3[...] + b3[...]).astype(BF)
    cot = cot_ref[0].reshape(m, D)
    out = after_row
    n3 = None
    for j in range(FF // FCH):
        cols = slice(j * FCH, (j + 1) * FCH)
        act, slope = gelu_pair(mm(low3, win[:, cols]))
        act = act.astype(BF)
        out = out + mm(act, wout[cols, :])
        ghid = (mt(cot, wout[cols, :]) * slope).astype(BF)
        aout[:, cols] += tm(cot, act)
        ain[:, cols] += tm(low3, ghid)
        back = mt(ghid, win[:, cols])
        n3 = back if n3 is None else n3 + back
    keep(3, 4)
    out_ref[0] = out.astype(BF).reshape(FB, rows, D)
    dg3[...] += fold8(n3 * xhat3)
    db3[...] += fold8(n3)
    g_row = cot.astype(F32) + norm_back(n3, xhat3, rstd3, g3[...])
    gb = g_row.astype(BF)
    settle(0, 1, 2)
    aro[...] += tm(heads, gb)
    gh2_s[...] = mt(gb, wro[...]).astype(BF)
    for g0 in range(0, len(jobs), GRP2):
        some = jobs[g0 : g0 + GRP2]
        gs = [gh2_s[at(f, h, 0)] for f, h in some]
        ps = [p_s[f * HEADS + h] for f, h in some]
        dps = [mt(g, qkv_s[at(f, h, 2)]) for g, (f, h) in zip(gs, some)]
        pds = [p.astype(F32) * dp for p, dp in zip(ps, dps)]
        dss = [(pd - p.astype(F32) * jnp.sum(pd, axis=-1, keepdims=True)).astype(BF) for p, pd in zip(ps, pds)]
        for (f, h), g, p, ds in zip(some, gs, ps, dss):
            gq_s[at(f, h, 2)] = tm(p, g).astype(BF)
            gq_s[at(f, h, 0)] = (mm(ds, qkv_s[at(f, h, 1)]) * SCALE).astype(BF)
            gq_s[at(f, h, 1)] = (tm(ds, qkv_s[at(f, h, 0)]) * SCALE).astype(BF)
    gq = gq_s[...]
    arq[...] += tm(low2, gq)
    n2 = mt(gq, wrq[...])
    dg2[...] += fold8(n2 * xhat2)
    db2[...] += fold8(n2)
    g_feat = g_row + norm_back(n2, xhat2, rstd2, g2[...])
    gaf_ref[...] = g_feat.reshape(FB, rows, D)
    gf = g_feat.astype(BF)
    afo[...] += tm(h1, gf)
    keep(0, 1, 2)
    h1_s[...] = mt(gf, wfo[...]).astype(BF)
    for k in range(n):
        for f in range(FB):
            for c, (r0, r1) in enumerate(spans):
                off = pl.multiple_of((me ^ k) * part + r0, 16)
                gh_refs[c * n + k][f] = h1_s[pl.ds(f * rows + off, r1 - r0), :]

    @pl.when(i == pl.num_programs(0) - 1)
    def _():
        if not last:
            for j in range(5):
                pltpu.make_async_copy(accs[j], kept[j], asems.at[j]).wait()
        else:
            core = core_ref[0]
            at = 0
            for acc in accs[:4]:
                for j in range(acc.shape[1] // D):
                    for b in range(D // (2 * ROWS_P)):
                        for side, ref in ((core, kept[0]), (1 - core, kept[1])):
                            row = pl.multiple_of((2 * b + side) * ROWS_P, ROWS_P)
                            ref[b, at : at + ROWS_P, :] = acc[pl.ds(row, ROWS_P), j * D : (j + 1) * D].astype(BF)
                    at += ROWS_P
            for j in range(FF // D):
                unit = jnp.where(lax.broadcasted_iota(jnp.int32, (D, D), 0) == lax.broadcasted_iota(jnp.int32, (D, D), 1), 1.0, 0.0)
                turned = mt(unit.astype(BF), aout[:, j * D : (j + 1) * D].astype(BF)).astype(BF).reshape(4, 2, 4 * ROWS_P, D)
                even, odd = turned[:, 0], turned[:, 1]
                blocks = slice(j * 4, (j + 1) * 4)
                kept[0][blocks, at:, :] = jnp.where(core == 0, even, odd)
                kept[1][blocks, at:, :] = jnp.where(core == 0, odd, even)


def middle(me, core, x, hs, cot, bias, pack, g2, b2, g3, b3, f0, spans, carried, last):
    n = len(hs)
    _, feats, rows, _ = x.shape
    part = rows // n
    m = FB * rows
    count = hs[0].shape[0]
    first = not carried
    any_ = pl.BlockSpec(memory_space=pl.ANY)
    xblk = pl.BlockSpec((1, FB, rows, D), lambda i, *_: (0, i + f0 // FB, 0, 0))
    hblk = lambda r: pl.BlockSpec((FB, r, D), lambda i, *_: (i, 0, 0))
    sds = jax.ShapeDtypeStruct
    sums = [(D, D), (D, QKV), (D, D), (D, FF), (D, FF)]
    half = (pack.shape[0] // 2,) + pack.shape[1:]
    kept_specs = [pl.BlockSpec(half, lambda i, *_: (0, 0, 0))] * 2 if last else [any_] * 5
    kept_shape = [sds(half, BF)] * 2 if last else [sds(q, F32) for q in sums]
    args = [x, *hs, cot, bias, pack, g2, b2, g3, b3, *carried]
    return pl.pallas_call(
        lambda *r: middle_kernel(*r, n=n, rows=rows, part=part, spans=spans, first=first, last=last),
        grid_spec=pltpu.PrefetchScalarGridSpec(
            num_scalar_prefetch=2,
            grid=(count // FB,),
            in_specs=[xblk]
            + [hblk(part)] * n
            + [xblk, full((rows, rows)), any_, full((1, D)), full((1, D)), full((1, D)), full((1, D))]
            + ([] if first else [any_] * 5 + [full((8, D))] * 4 + [any_] * 2),
            out_specs=[xblk, pl.BlockSpec((FB, rows, D), lambda i, *_: (i + f0 // FB, 0, 0))]
            + [hblk(r1 - r0) for r0, r1 in spans for _ in range(n)]
            + kept_specs
            + [pl.BlockSpec((8, D), lambda i, *_: (0, 0))] * 4,
            scratch_shapes=[
                pltpu.VMEM((m, D), BF),
                pltpu.VMEM((m, QKV), BF),
                pltpu.VMEM((FB * HEADS, rows, rows), BF),
                pltpu.VMEM((m, QKV), BF),
                pltpu.VMEM((m, D), BF),
                pltpu.VMEM((m, D), BF),
            ]
            + [pltpu.VMEM(q, F32) for q in sums]
            + [
                pltpu.VMEM((32, ROWS_P, D), BF),
                pltpu.VMEM((32, ROWS_P, QKV), BF),
                pltpu.VMEM((32, ROWS_P, D), BF),
                pltpu.VMEM((32, ROWS_P, FF), BF),
                pltpu.VMEM((32, 4 * ROWS_P, D), BF),
                pltpu.SemaphoreType.DMA((10,)),
                pltpu.SemaphoreType.DMA((5,)),
            ],
        ),
        out_shape=[sds(x.shape, BF), sds((feats, rows, D), F32)]
        + [sds((count, r1 - r0, D), BF) for r0, r1 in spans for _ in range(n)]
        + kept_shape
        + [sds((8, D), F32)] * 4,
        input_output_aliases={} if first else {2 + len(args) - 2: 0, 2 + len(args) - 1: 1},
        compiler_params=pltpu.CompilerParams(vmem_limit_bytes=VMEM),
        cost_estimate=COST,
        name="middle",
    )(me, core, *args)


def final_kernel(me_ref, g_ref, *refs, n):
    out = refs[-1]
    for k in range(n):

        @pl.when(pl.program_id(0) == k)
        def _():
            out[0] = g_ref[...] + refs[k][...].astype(F32)


def final(me, g, ds, r0, before):
    n = len(ds)
    feats, rows, _ = g.shape
    count = ds[0].shape[1]
    each = rows // n // count
    place = lambda i, me: (me[0] ^ i) * each + r0 // count
    more = [] if before is None else [before]
    return pl.pallas_call(
        lambda *r: final_kernel(*r, n=n),
        grid_spec=pltpu.PrefetchScalarGridSpec(
            num_scalar_prefetch=1,
            grid=(n,),
            in_specs=[pl.BlockSpec((feats, count, D), lambda i, me: (0, place(i, me), 0))]
            + [full((feats, count, D))] * n
            + [pl.BlockSpec(memory_space=pl.ANY)] * len(more),
            out_specs=pl.BlockSpec((1, feats, count, D), lambda i, me: (0, 0, place(i, me), 0)),
        ),
        out_shape=jax.ShapeDtypeStruct((1, feats, rows, D), F32),
        input_output_aliases={2 + n: 0} if more else {},
        compiler_params=pltpu.CompilerParams(vmem_limit_bytes=VMEM),
        cost_estimate=COST,
        name="final",
    )(me, g, *ds, *more)


def pack_kernel(*refs):
    vectors, qkv, *mats, down, first, pack = refs
    first[:, :QKV] = qkv[...]
    r = qkv.shape[0]
    first[:, QKV:] = jnp.broadcast_to(vectors[...], (r, 128))
    at = 0
    for m in mats:
        for j in range(m.shape[1] // D):
            pack[at : at + r] = m[:, j * D : (j + 1) * D]
            at += r
    pack[at:] = down[...]


def pack_shards(vectors, qkv, mats, down):
    r = qkv.shape[0]
    if r % ROWS_P:
        pack = jnp.concatenate([m[:, j * D : (j + 1) * D] for m in mats for j in range(m.shape[1] // D)] + [down], axis=0)
        return jnp.concatenate([qkv, jnp.broadcast_to(vectors, (r, 128))], axis=1), pack
    return pl.pallas_call(
        pack_kernel, out_shape=[jax.ShapeDtypeStruct((r, QKV + 128), BF), jax.ShapeDtypeStruct((13 * r, D), BF)], name="pack"
    )(vectors, qkv, *mats, down)


def row_allowed(segments, context):
    tables = jnp.arange(context.shape[0], dtype=jnp.int32)
    member = (segments[:, None] == tables[None, :]).astype(jnp.int32)
    sizes = jnp.sum(member, axis=0)
    starts = jnp.cumsum(sizes) - sizes
    places = jnp.arange(segments.shape[0], dtype=jnp.int32) - jnp.sum(member * starts[None, :], axis=1)
    limits = jnp.sum(member * context[None, :], axis=1)
    usable = places < limits
    return (segments[:, None] == segments[None, :]) & usable[None, :]


def swap(arrays, n):
    return [arrays[0]] + [lax.ppermute(arrays[k], "feat", [(d, d ^ k) for d in range(n)]) for k in range(1, n)]


def exchange(x, me, n, after):
    feats, rows, _ = x.shape

    def move(a, at, rows, bit):
        low = ((me // bit) % 2) * rows
        sent = lax.dynamic_slice(a, (0, at + rows - low, 0), (feats, rows, D))
        if bit == n // 2:
            sent, _ = together(sent, after)
        return lax.ppermute(sent, "feat", [(d, d ^ bit) for d in range(n)]), at + low

    bit = n // 2
    got, low = move(x, 0, rows // 2, bit)
    got = [got]

    def finish():
        have, places, half, bit = [(x, low), (got[0], 0)], [0, n // 2], rows // 2, n // 4
        while bit:
            half //= 2
            moved = [move(a, at, half, bit) for a, at in have]
            have = [(a, at) for (a, _), (_, at) in zip(have, moved)] + [(a, 0) for a, _ in moved]
            places = places + [q ^ bit for q in places]
            bit //= 2
        return [have[places.index(k)] for k in range(n)]

    return got, finish


class Shards:
    def __init__(self, rows, n):
        self.count = rows * n
        self.bits = [("rows", 1 << b) for b in reversed(range(rows.bit_length() - 1))]
        self.bits += [("feat", 1 << b) for b in reversed(range(n.bit_length() - 1))]
        self.sizes = {"rows": rows, "feat": n}
        last = len(self.bits) - 1
        self.rows_bits = list(range(rows.bit_length() - 1))
        self.near = last
        self.feat_bits = list(range(rows.bit_length() - 1, last))

    def other(self, a, at):
        axis, bit = self.bits[at]
        return lax.ppermute(a, axis, [(d, d ^ bit) for d in range(self.sizes[axis])])

    def side(self, at):
        axis, bit = self.bits[at]
        return (lax.axis_index(axis) // bit) % 2

    def gather(self, a, order):
        if a.ndim == 2:
            a = a.reshape((1,) * len(self.bits) + a.shape)
        while order:
            at, *rest = order
            if rest and rest[0] == at + 1 and self.bits[at][0] == "rows" == self.bits[at + 1][0] and self.sizes["rows"] <= 8:
                a = self.gather_two(a, at)
                order = rest[1:]
                continue
            b = self.other(a, at)
            low = self.side(at) == 0
            a = jnp.concatenate([jnp.where(low, a, b), jnp.where(low, b, a)], axis=at)
            order = rest
        return a

    def gather_two(self, a, at):
        axis, high = self.bits[at]
        low = self.bits[at + 1][1]
        move = lambda mask: lax.ppermute(a, axis, [(d, d ^ mask) for d in range(self.sizes[axis])])
        all_ = [[a, move(low)], [move(high), move(high | low)]]
        line = lambda q, side: jnp.concatenate([jnp.where(side, q[1], q[0]), jnp.where(side, q[0], q[1])], axis=at + 1)
        q = [line(pair, self.side(at + 1) == 1) for pair in all_]
        side = self.side(at) == 1
        return jnp.concatenate([jnp.where(side, q[1], q[0]), jnp.where(side, q[0], q[1])], axis=at)

    def spread(self, a):
        return a.reshape((2,) * len(self.bits) + a.shape[1:])

    def halve(self, a, at):
        side = self.side(at)
        return lax.dynamic_index_in_dim(a, side, at, True), lax.dynamic_index_in_dim(a, 1 - side, at, True)

    def quarter(self, a, at):
        high, low = self.side(at), self.side(at + 1)
        pick = lambda i, j: lax.dynamic_index_in_dim(lax.dynamic_index_in_dim(a, i, at, True), j, at + 1, True)
        return pick(high, low), [pick(high, 1 - low), pick(1 - high, low), pick(1 - high, 1 - low)]

    def others(self, parts, at):
        axis, high = self.bits[at]
        low = self.bits[at + 1][1]
        masks = (low, high, high | low)
        return [lax.ppermute(a, axis, [(d, d ^ mask) for d in range(self.sizes[axis])]) for a, mask in zip(parts, masks)]

    def step(self, a, at, held=BF):
        mine, others = self.halve(a, at)
        return (mine.astype(F32) + self.other(others, at).astype(F32)).astype(held)

    def scatter(self, a, order):
        for at in order[:-1]:
            a = self.step(a, at)
        a = self.step(a, order[-1], F32)
        return a.reshape(a.shape[-2:])


def begin(shards, sums, ats):
    halves = [shards.halve(a, at) for a, at in zip(sums, ats)]
    return [mine for mine, _ in halves], [shards.other(others, at) for (_, others), at in zip(halves, ats)]


def add(mine, got, held=BF):
    return [(a.astype(F32) + b.astype(F32)).astype(held) for a, b in zip(mine, got)]


def together(a, b):
    return lax.optimization_barrier((a, b))


def repack(a, blocks):
    count = a.shape[0]
    if count == blocks:
        return a
    r, q = D // count, D // blocks
    parts = [a[:, j * r : (j + 1) * r].reshape(blocks, q, D) for j in range(9)]
    return jnp.concatenate(parts + [a[:, 9 * r :].reshape(blocks, 4 * q, D)], axis=1)


def per_device(rows_axis, n, inputs, *rest):
    weights, (cotangent, segments, context, feature_mask) = rest[:12], rest[12:]
    gain_one, shift_one, qkv_one, out_one, gain_two, shift_two, qkv_two, out_two, gain_three, shift_three, up, down = weights
    shards = Shards(rows_axis, n)
    _, feats, rows, _ = inputs.shape
    part = rows // n
    tot = n * feats
    me = lax.axis_index("feat").astype(jnp.int32)
    me_arr = me.reshape(1)

    core = (me % 2).reshape(1)
    vectors = (gain_one, shift_one, gain_two, shift_two, gain_three, shift_three)
    r = D // shards.count
    vectors = sum(jnp.pad(v, (j * r, 128 - (j + 1) * r)) for j, v in enumerate(vectors)).reshape(1, 128)
    first, pack = pack_shards(vectors, qkv_one, (out_one, qkv_two, out_two, up), down)
    pack = repack(lax.all_gather(pack, ("rows", "feat"), axis=0), D // ROWS_P)
    first = shards.gather(first, shards.feat_bits[:1])
    got, xs_at = exchange(inputs[0], me, n, first)
    first = shards.gather(first, shards.feat_bits[1:] + shards.rows_bits)
    got[0], first = together(got[0], first)
    xs_at = xs_at()
    first = shards.gather(first, [shards.near]).reshape(D, QKV + 128)
    gains = first.reshape(shards.count, r, QKV + 128)[:, 0, QKV : QKV + 6 * r].reshape(shards.count, 6, r)
    gains = gains.transpose(1, 0, 2).reshape(6, D).astype(F32)
    g1, b1, g2, b2, g3, b3 = [gains[j : j + 1] for j in range(6)]

    xs = [a for a, _ in xs_at]
    x_rows = jnp.stack([jnp.asarray(at, jnp.int32) for _, at in xs_at]) // RC
    order = me ^ jnp.arange(n, dtype=jnp.int32)
    valid = jnp.take(feature_mask[0].reshape(n, feats), order, axis=0).reshape(tot) > 0
    wide = -(-2 * tot // 128) * 128
    lane = jnp.arange(wide)
    same = (lane[None, :] // tot == jnp.arange(2 * tot)[:, None] // tot) & (lane < 2 * tot)[None, :]
    bias_one = jnp.where(same & jnp.pad(jnp.tile(valid, 2), (0, wide - 2 * tot))[None, :], 0.0, MASKED).astype(F32)
    bias_two = jnp.where(row_allowed(segments[0], context[0]), 0.0, MASKED).astype(F32)

    cut = feats // 2
    cuts = ((0, cut), (cut, feats))
    half = part // 2
    res = feature_forward(x_rows, xs, g1, b1, first, bias_one, cuts, part)
    qkv, p = res[2 * n :]
    h_a, h_b = swap(res[:n], n), swap(res[n : 2 * n], n)
    gains_two = (g2, b2, g3, b3)
    res = middle(me_arr, core, inputs, h_a, cotangent, bias_two, pack, *gains_two, 0, ((0, part),), [], False)
    output, gaf, carried = res[0], res[1], res[2 + n :]
    g_a = swap(res[2 : 2 + n], n)
    spans = ((0, half), (half, part))
    res = middle(me_arr, core, inputs, h_b, cotangent, bias_two, pack, *gains_two, cut, spans, [*carried, output, gaf], True)
    g_a, res = together(g_a, res)
    output, gaf = res[:2]
    g_b, g_c = swap(res[2 : 2 + n], n), swap(res[2 + n : 2 + 2 * n], n)
    mine, others, *vector_grads = res[2 + 2 * n :]

    wide_first, tall_first = shards.rows_bits[::-1], shards.rows_bits[-2::-1] + shards.rows_bits[-1:]
    if shards.count == D // ROWS_P:
        dpack = (mine.astype(F32) + shards.other(others, shards.near).astype(F32)).astype(BF)
        dpack = dpack.reshape((2,) * (len(shards.bits) - 1) + (1,) + dpack.shape[1:])
    else:
        dpack = jnp.where(core[0] == 0, jnp.stack((mine, others), 1), jnp.stack((others, mine), 1))
        dpack = shards.step(shards.spread(repack(dpack.reshape(pack.shape), shards.count)), shards.near)
    g_b, dpack = together(g_b, dpack)
    share = dpack.shape[-2] // 2 // ROWS_P * ROWS_P
    two = [dpack[..., :share, :], dpack[..., share:, :]]
    ways = [wide_first + shards.feat_bits, tall_first + shards.feat_bits]

    mine, got = begin(shards, two, [way[0] for way in ways])
    *d_a, acc, dg1, db1 = feature_backward(
        x_rows, xs, [(0, g_a), (0, g_b)], qkv, p, g1, b1, first, cuts, 0, half, [], []
    )
    got, d_a, g_c = lax.optimization_barrier((got, d_a, g_c))
    two = add(mine, got)
    two, g_c = together(two, g_c)

    mine, got = begin(shards, two, [way[1] for way in ways])
    d_a = swap(d_a, n)
    *d_b, dfirst = feature_backward(
        x_rows, xs, [(0, g_a), (half, g_c)], qkv, p, g1, b1, first, cuts, half, part, [acc, dg1, db1], vector_grads
    )
    got, d_a, d_b, dfirst = lax.optimization_barrier((got, d_a, d_b, dfirst))
    d_b = swap(d_b, n)
    dfirst = shards.step(shards.spread(dfirst.reshape(shards.count, -1, QKV + 128)), shards.near)
    two = add(mine, got)
    for i in range(2, len(ways[0]) - 2):
        two = add(*begin(shards, two, [way[i] for way in ways]))
    d_a, dfirst = together(d_a, dfirst)

    mine, got = begin(shards, [*two, dfirst], [way[-2] for way in ways] + wide_first[:1])
    input_grad = final(me_arr, gaf, d_a, 0, None)
    got, input_grad = together(got, input_grad)
    *two, dfirst = add(mine, got)
    last = wide_first[1:] + shards.feat_bits
    if len(last) == 3:
        two, dfirst = together(two, dfirst)
        mine, got = begin(shards, two, [way[-1] for way in ways])
        kept, others = shards.quarter(dfirst, last[1])
        others, d_b, got = lax.optimization_barrier((shards.others(others, last[1]), d_b, got))
        input_grad = final(me_arr, gaf, d_b, half, input_grad)
        others, input_grad, got = lax.optimization_barrier((others, input_grad, got))
        dfirst = sum([b.astype(F32) for b in others], kept.astype(F32)).astype(BF)
        last = last[2:]
    else:
        input_grad = final(me_arr, gaf, d_b, half, input_grad)
        mine, got = begin(shards, two, [way[-1] for way in ways])
    dpack = jnp.concatenate([a.reshape(a.shape[-2:]) for a in add(mine, got, F32)])
    dfirst = shards.scatter(dfirst, last)
    piece = lambda a, b: jnp.concatenate([dpack[j * r : (j + 1) * r] for j in range(a, b)], axis=1)
    v = [dfirst[:, QKV + j] for j in range(6)]
    return (
        output,
        input_grad,
        v[0],
        v[1],
        dfirst[:, :QKV],
        piece(0, 1),
        v[2],
        v[3],
        piece(1, 4),
        piece(4, 5),
        v[4],
        v[5],
        piece(5, 9),
        dpack[9 * r :],
    )


def solution(mesh):
    rows_axis, n = mesh.shape["rows"], mesh.shape["feat"]
    vec, mat, act, tab = P(("rows", "feat")), P(("rows", "feat"), None), P("rows", "feat", None, None), P("rows", None)
    weights = (vec, vec, mat, mat, vec, vec, mat, mat, vec, vec, mat, mat)
    return jax.shard_map(
        lambda *a: per_device(rows_axis, n, *a),
        mesh=mesh,
        in_specs=(act,) + weights + (act, tab, tab, tab),
        out_specs=(act, act) + weights,
        check_vma=False,
    )
```

```python
import math

import jax
import jax.numpy as jnp
import numpy as np
from jax import lax
from jax.experimental import pallas as pl
from jax.experimental.pallas import tpu as pltpu
from jax.sharding import PartitionSpec as P

D = 512
HEADS = 4
HEAD_DIM = 128
FF = 2048
QKV = 3 * D
EPS = 1e-05
MASKED = -1e30
SCALE = HEAD_DIM**-0.5
BF = jnp.bfloat16
F32 = jnp.float32
LOG2E = float(np.log2(np.e))
VMEM = 60 * 1024 * 1024

GRP2 = 8
GRP = 4
SHARE = 112
ROWS_P = 16
COST = pl.CostEstimate(flops=10**11, bytes_accessed=10**6, transcendentals=0)
RC = 16
FCH = 256
FB = 2


def mm(a, b):
    return lax.dot_general(a, b, (((1,), (0,)), ((), ())), preferred_element_type=F32)


def mt(a, b):
    return lax.dot_general(a, b, (((1,), (1,)), ((), ())), preferred_element_type=F32)


def tm(a, b):
    return lax.dot_general(a, b, (((0,), (0,)), ((), ())), preferred_element_type=F32)


def norm(x):
    mean = jnp.mean(x, axis=-1, keepdims=True)
    centred = x - mean
    var = jnp.mean(centred * centred, axis=-1, keepdims=True)
    rstd = lax.rsqrt(var + EPS)
    return centred * rstd, rstd


def norm_back(n, xhat, rstd, gain):
    e = n * gain
    m1 = jnp.mean(e, axis=-1, keepdims=True)
    m2 = jnp.mean(e * xhat, axis=-1, keepdims=True)
    return rstd * (e - m1 - xhat * m2)


def fold8(a):
    return jnp.sum(a.reshape(a.shape[0] // 8, 8, a.shape[1]), axis=0)


def gelu_pair(h):
    e = jnp.exp2(h * h * (-0.5 * LOG2E))
    d = 1.0 + (0.3275911 * 2**-0.5) * jnp.abs(h)
    t = pl.reciprocal(d, approx=True)
    t = t * (2.0 - d * t)
    poly = 0.5 * 1.061405429
    for c in (-1.453152027, 1.421413741, -0.284496736, 0.254829592):
        poly = poly * t + 0.5 * c
    q = poly * t * e
    cdf = jnp.where(h >= 0, 1.0 - q, q)
    return h * cdf, cdf + h * e * (2 * np.pi) ** -0.5


def by_rows(parts):
    a = jnp.swapaxes(jnp.concatenate(parts, axis=0), 0, 1)
    return a.reshape(a.shape[0] * a.shape[1], D)


def by_features(a, tot):
    return jnp.swapaxes(a.reshape(a.shape[0] // tot, tot, D), 0, 1)


def full(shape):
    return pl.BlockSpec(shape, lambda *_: (0,) * len(shape), pipeline_mode=pl.Buffered(1))


def feature_forward_kernel(_, *refs, n, feats, cuts):
    x_refs, (gain, shift, wqkv, bias), outs = refs[:n], refs[n : n + 4], refs[n + 4 :]
    nc = n * len(cuts)
    h_refs, (qkv_ref, p_ref), (xs, low, hs) = outs[:nc], outs[nc : nc + 2], outs[nc + 2 :]
    tot = n * feats
    pair = 2 * tot
    wide = bias.shape[1]
    xs[...] = by_rows([x_refs[k][...] for k in range(n)])
    for r in range(RC):
        at = slice(r * tot, (r + 1) * tot)
        xhat, _ = norm(xs[at].astype(F32))
        low[at] = (xhat * gain[...] + shift[...]).astype(BF)
    rows = tot * RC
    qkv_ref[0, :rows] = mm(low[...], wqkv[...]).astype(BF)
    qkv_ref[0, rows:] = jnp.zeros((qkv_ref.shape[1] - rows, QKV), BF)
    mask = bias[...]
    for b0 in range(0, RC // 2, GRP):
        jobs = [(b, h) for b in range(b0, b0 + GRP) for h in range(HEADS)]
        at = lambda b, h, c, w: (0, slice(b * pair, b * pair + w), slice(c * D + h * 128, c * D + h * 128 + 128))
        ss = [mt(qkv_ref[at(b, h, 0, pair)], qkv_ref[at(b, h, 1, wide)]) * (SCALE * LOG2E) + mask for b, h in jobs]
        es = [jnp.exp2(s - jnp.max(s, axis=-1, keepdims=True)) for s in ss]
        ps = [(e * (1.0 / jnp.sum(e, axis=-1, keepdims=True))).astype(BF) for e in es]
        os = [mm(p, qkv_ref[at(b, h, 2, wide)]) for p, (b, h) in zip(ps, jobs)]
        for p, o, (b, h) in zip(ps, os, jobs):
            p_ref[0, b, h] = p
            hs[b * pair : (b + 1) * pair, h * 128 : h * 128 + 128] = o.astype(BF)
    heads = by_features(hs[...], tot)
    for c, (f0, f1) in enumerate(cuts):
        for k in range(n):
            h_refs[c * n + k][...] = heads[k * feats + f0 : k * feats + f1]


def feature_forward(x_rows, xs, gain, shift, wqkv, bias, cuts, rows):
    n = len(xs)
    feats = xs[0].shape[0]
    tot = n * feats
    steps = rows // RC
    pad = tot * RC - 2 * tot + bias.shape[1]
    sds = jax.ShapeDtypeStruct
    return pl.pallas_call(
        lambda *r: feature_forward_kernel(*r, n=n, feats=feats, cuts=cuts),
        grid_spec=pltpu.PrefetchScalarGridSpec(
            num_scalar_prefetch=1,
            grid=(steps,),
            in_specs=[pl.BlockSpec((feats, RC, D), lambda i, at, k=k: (0, i + at[k], 0)) for k in range(n)]
            + [full((1, D)), full((1, D)), full((D, QKV)), full(bias.shape)],
            out_specs=[pl.BlockSpec((f1 - f0, RC, D), lambda i, at: (0, i, 0)) for f0, f1 in cuts for _ in range(n)]
            + [
                pl.BlockSpec((1, pad, QKV), lambda i, at: (i, 0, 0)),
                pl.BlockSpec((1, RC // 2, HEADS, 2 * tot, bias.shape[1]), lambda i, at: (i, 0, 0, 0, 0)),
            ],
            scratch_shapes=[
                pltpu.VMEM((tot * RC, D), BF),
                pltpu.VMEM((tot * RC, D), BF),
                pltpu.VMEM((tot * RC, D), BF),
            ],
        ),
        out_shape=[sds((f1 - f0, rows, D), BF) for f0, f1 in cuts for _ in range(n)]
        + [sds((steps, pad, QKV), BF), sds((steps, RC // 2, HEADS, 2 * tot, bias.shape[1]), BF)],
        compiler_params=pltpu.CompilerParams(vmem_limit_bytes=VMEM),
        cost_estimate=COST,
        name="feature_forward",
    )(x_rows, *xs, gain, shift, wqkv, bias)


def feature_backward_kernel(at_ref, *refs, n, feats, cuts, first, last):
    it = iter(refs)
    take = lambda c: [next(it) for _ in range(c)]
    x_refs = take(n)
    g_refs = take(n * len(cuts))
    qkv_ref, p_ref, gain, shift, wqkv = take(5)
    carried = [] if first else take(3)
    others = take(4) if last else []
    d_refs = take(n)
    outs = take(2) if last else take(3)
    dgain, dshift, vecs, xs, xh, rs, ns, low, gh, gqkv, acc = take(11)
    if not last:
        acc, dgain, dshift = outs
    tot = n * feats
    pair = 2 * tot
    wide = p_ref.shape[-1]
    i = pl.program_id(0)

    @pl.when(i == 0)
    def _():
        for j, a in enumerate((acc, dgain, dshift)):
            a[...] = jnp.zeros_like(a) if first else carried[j][...]

    xs[...] = by_rows([x_refs[k][...] for k in range(n)])
    gh[...] = by_rows([g_refs[c * n + k][...] for k in range(n) for c in range(len(cuts))])
    for r in range(RC):
        at = slice(r * tot, (r + 1) * tot)
        xhat, rstd = norm(xs[at].astype(F32))
        xh[at] = xhat
        rs[at] = jnp.broadcast_to(rstd, (tot, 128))
        low[at] = (xhat * gain[...] + shift[...]).astype(BF)
    for b0 in range(0, RC // 2, GRP):
        jobs = [(b, h) for b in range(b0, b0 + GRP) for h in range(HEADS)]
        at = lambda b, h, c, w: (0, slice(b * pair, b * pair + w), slice(c * D + h * 128, c * D + h * 128 + 128))
        gs_ = [gh[b * pair : (b + 1) * pair, h * 128 : h * 128 + 128] for b, h in jobs]
        dps = [mt(g, qkv_ref[at(b, h, 2, wide)]) for g, (b, h) in zip(gs_, jobs)]
        ps = [p_ref[0, b, h] for b, h in jobs]
        dvs = [tm(p, g) for p, g in zip(ps, gs_)]
        pds = [p.astype(F32) * dp for p, dp in zip(ps, dps)]
        dss = [(pd - p.astype(F32) * jnp.sum(pd, axis=-1, keepdims=True)).astype(BF) for p, pd in zip(ps, pds)]
        dqs = [mm(ds, qkv_ref[at(b, h, 1, wide)]) for ds, (b, h) in zip(dss, jobs)]
        dks = [tm(ds, qkv_ref[at(b, h, 0, pair)]) for ds, (b, h) in zip(dss, jobs)]
        for (b, h), dq, dk, dv in zip(jobs, dqs, dks, dvs):
            span = slice(b * pair, (b + 1) * pair)
            gqkv[span, h * 128 : h * 128 + 128] = (dq * SCALE).astype(BF)
            gqkv[span, D + h * 128 : D + h * 128 + 128] = (dk * SCALE).astype(BF)[:pair]
            gqkv[span, 2 * D + h * 128 : 2 * D + h * 128 + 128] = dv.astype(BF)[:pair]
    acc[...] += tm(low[...], gqkv[...])
    ns[...] = mt(gqkv[...], wqkv[...])
    for r in range(RC):
        at = slice(r * tot, (r + 1) * tot)
        xhat = xh[at]
        nn = ns[at]
        dgain[...] += fold8(nn * xhat)
        dshift[...] += fold8(nn)
        xs[at] = norm_back(nn, xhat, rs[at, :1], gain[...]).astype(BF)
    back = by_features(xs[...], tot)
    for k in range(n):
        d_refs[k][...] = back[k * feats : (k + 1) * feats]

    if last:

        @pl.when(i == pl.num_programs(0) - 1)
        def _():
            core = at_ref[n]
            vecs[...] = jnp.zeros_like(vecs)
            for j, v in enumerate([dgain, dshift] + others):
                vecs[j : j + 1] = jnp.sum(v[...], axis=0, keepdims=True)
            turned = vecs[...].T.astype(BF).reshape(D // (2 * ROWS_P), 2, ROWS_P, 128)
            outs[0][:, :, QKV:] = jnp.where(core == 0, turned[:, 0], turned[:, 1])
            outs[1][:, :, QKV:] = jnp.where(core == 0, turned[:, 1], turned[:, 0])
            for b in range(D // (2 * ROWS_P)):
                for side, ref in ((core, outs[0]), (1 - core, outs[1])):
                    row = pl.multiple_of((2 * b + side) * ROWS_P, ROWS_P)
                    ref[b, :, :QKV] = acc[pl.ds(row, ROWS_P), :].astype(BF)


def feature_backward(x_rows, xs, gs, qkv, p, gain, shift, wqkv, cuts, r0, r1, carried, others):
    n = len(xs)
    feats = xs[0].shape[0]
    tot = n * feats
    s0, steps = r0 // RC, (r1 - r0) // RC
    first, last = not carried, bool(others)
    sds = jax.ShapeDtypeStruct
    at = lambda f, row: pl.BlockSpec((f, RC, D), lambda i, _: (0, i + (r0 - row) // RC, 0))
    sums = [(D, QKV), (8, D), (8, D)]
    if last:
        each = (D // (2 * ROWS_P), ROWS_P, QKV + 128)
        out_specs, out_shape = [pl.BlockSpec(each, lambda i, _: (0, 0, 0))] * 2, [sds(each, BF)] * 2
    else:
        out_specs, out_shape = [pl.BlockSpec(q, lambda i, _: (0, 0)) for q in sums], [sds(q, F32) for q in sums]
    return pl.pallas_call(
        lambda *r: feature_backward_kernel(*r, n=n, feats=feats, cuts=cuts, first=first, last=last),
        grid_spec=pltpu.PrefetchScalarGridSpec(
            num_scalar_prefetch=1,
            grid=(steps,),
            in_specs=[pl.BlockSpec((feats, RC, D), lambda i, q, k=k: (0, i + s0 + q[k], 0)) for k in range(n)]
            + [at(f1 - f0, row) for (f0, f1), (row, _) in zip(cuts, gs) for _ in range(n)]
            + [
                pl.BlockSpec((1,) + qkv.shape[1:], lambda i, _: (i + s0, 0, 0)),
                pl.BlockSpec((1,) + p.shape[1:], lambda i, _: (i + s0, 0, 0, 0, 0)),
                full((1, D)),
                full((1, D)),
                full((D, QKV)),
            ]
            + [full(q.shape) for q in carried]
            + [full((8, D)) for _ in others],
            out_specs=[at(feats, r0)] * n + out_specs,
            scratch_shapes=[
                pltpu.VMEM((8, D), F32),
                pltpu.VMEM((8, D), F32),
                pltpu.VMEM((128, D), F32),
                pltpu.VMEM((tot * RC, D), BF),
                pltpu.VMEM((tot * RC, D), F32),
                pltpu.VMEM((tot * RC, 128), F32),
                pltpu.VMEM((tot * RC, D), F32),
                pltpu.VMEM((tot * RC, D), BF),
                pltpu.VMEM((tot * RC, D), BF),
                pltpu.VMEM((tot * RC, QKV), BF),
                pltpu.VMEM((D, QKV), F32),
            ],
        ),
        out_shape=[sds((feats, r1 - r0, D), BF)] * n + out_shape,
        compiler_params=pltpu.CompilerParams(vmem_limit_bytes=VMEM),
        cost_estimate=COST,
        name="feature_backward",
    )(x_rows, *xs, *[a for _, part in gs for a in part], qkv, p, gain, shift, wqkv, *carried, *others)


class Flat:
    def __init__(self, ref):
        self.ref = ref

    def __getitem__(self, key):
        rows, cols = (slice(None), slice(None)) if key is Ellipsis else key
        r = self.ref.shape[1]
        if rows.start is not None:
            rows = slice(rows.start // r, rows.stop // r)
        w = self.ref[rows, :, cols]
        return w.reshape(w.shape[0] * w.shape[1], w.shape[2])


def unpack_copies(pack, weights, sems):
    copies, at = [], 0
    for w in weights:
        r = w.shape[1]
        for j in range(w.shape[2] // D):
            src = pack.at[:, pl.ds(at, r), :]
            copies.append(pltpu.make_async_copy(src, w.at[:, :, pl.ds(j * D, D)], sems.at[len(copies)]))
            at += r
    return copies


def middle_kernel(me_ref, core_ref, *refs, n, rows, part, spans, first):
    it = iter(refs)
    take = lambda c: [next(it) for _ in range(c)]
    (x_ref,) = take(1)
    h_refs = take(n)
    cot_ref, bias, pack, g2, b2, g3, b3 = take(7)
    carried = [] if first else take(6)
    _ = [] if first else take(2)
    out_ref, gaf_ref = take(2)
    gh_refs = take(n * len(spans))
    kept = take(2)
    dg2, db2, dg3, db3 = take(4)
    h1_s, qkv_s, p_s, gq_s, heads_s, gh2_s, afo, arq, aro, ain, aout, wfo_s, wrq_s, wro_s, win_s, wout_s, sems, asems = take(18)
    i = pl.program_id(0)
    me = me_ref[0]
    m = FB * rows
    accs = (afo, arq, aro, ain, aout)

    @pl.when(i == 0)
    def _():
        copies = unpack_copies(pack, (wfo_s, wrq_s, wro_s, win_s, wout_s), sems)
        for c in copies:
            c.start()
        for a in (afo, arq, aro, ain, aout):
            a[...] = jnp.zeros_like(a)
        for j, a in enumerate((dg2, db2, dg3, db3)):
            a[...] = jnp.zeros_like(a) if first else carried[2 + j][...]
        if not first:
            for j in range(2):
                pltpu.make_async_copy(carried[j], kept[j], asems.at[j]).start()

    def need(*which):
        @pl.when(i == 0)
        def _():
            at = 0
            for j, w in enumerate((wfo_s, wrq_s, wro_s, win_s, wout_s)):
                for _ in range(w.shape[2] // D):
                    if j in which:
                        pltpu.make_async_copy(pack.at[:, pl.ds(0, w.shape[1]), :], w.at[:, :, pl.ds(0, D)], sems.at[at]).wait()
                    at += 1

    wfo, wrq, wro, win, wout = (Flat(w) for w in (wfo_s, wrq_s, wro_s, win_s, wout_s))
    for k in range(n):
        off = pl.multiple_of((me ^ k) * part, part)
        for f in range(FB):
            h1_s[pl.ds(f * rows + off, part), :] = h_refs[k][f]
    x = x_ref[0].reshape(m, D).astype(F32)
    h1 = h1_s[...]
    need(0)
    after_feat = x + mm(h1, wfo[...])
    xhat2, rstd2 = norm(after_feat)
    low2 = (xhat2 * g2[...] + b2[...]).astype(BF)
    need(1, 2, 3, 4)
    qkv_s[...] = mm(low2, wrq[...]).astype(BF)
    mask = bias[...]
    jobs = [(f, h) for f in range(FB) for h in range(HEADS)]
    at = lambda f, h, c: (slice(f * rows, (f + 1) * rows), slice(c * D + h * 128, c * D + h * 128 + 128))
    for g0 in range(0, len(jobs), GRP2):
        some = jobs[g0 : g0 + GRP2]
        ss = [mt(qkv_s[at(f, h, 0)], qkv_s[at(f, h, 1)]) * (SCALE * LOG2E) + mask for f, h in some]
        es = [jnp.exp2(s - jnp.max(s, axis=-1, keepdims=True)) for s in ss]
        ps = [(e * (1.0 / jnp.sum(e, axis=-1, keepdims=True))).astype(BF) for e in es]
        for p, (f, h) in zip(ps, some):
            p_s[f * HEADS + h] = p
            heads_s[at(f, h, 0)] = mm(p, qkv_s[at(f, h, 2)]).astype(BF)
    heads = heads_s[...]
    after_row = after_feat + mm(heads, wro[...])
    xhat3, rstd3 = norm(after_row)
    low3 = (xhat3 * g3[...] + b3[...]).astype(BF)
    cot = cot_ref[0].reshape(m, D)
    out = after_row
    n3 = None
    chunks = [slice(j * FCH, (j + 1) * FCH) for j in range(FF // FCH)]
    hid = mm(low3, win[:, chunks[0]])
    gact = mt(cot, wout[chunks[0], :])
    waiting = None
    for j, cols in enumerate(chunks + [None]):
        if cols is not None:
            act, slope = gelu_pair(hid)
            act = act.astype(BF)
            ghid = (gact * slope).astype(BF)
            if j + 1 < len(chunks):
                hid = mm(low3, win[:, chunks[j + 1]])
                gact = mt(cot, wout[chunks[j + 1], :])
        if waiting is not None:
            a0, g0, c0 = waiting
            out = out + mm(a0, wout[c0, :])
            back = mt(g0, win[:, c0])
            n3 = back if n3 is None else n3 + back
            aout[:, c0] += tm(cot, a0)
            ain[:, c0] += tm(low3, g0)
        waiting = (act, ghid, cols)
    out_ref[0] = out.astype(BF).reshape(FB, rows, D)
    dg3[...] += fold8(n3 * xhat3)
    db3[...] += fold8(n3)
    g_row = cot.astype(F32) + norm_back(n3, xhat3, rstd3, g3[...])
    gb = g_row.astype(BF)
    gh2_s[...] = mt(gb, wro[...]).astype(BF)
    aro[...] += tm(heads, gb)
    for g0 in range(0, len(jobs), GRP2):
        some = jobs[g0 : g0 + GRP2]
        gs = [gh2_s[at(f, h, 0)] for f, h in some]
        ps = [p_s[f * HEADS + h] for f, h in some]
        dps = [mt(g, qkv_s[at(f, h, 2)]) for g, (f, h) in zip(gs, some)]
        pds = [p.astype(F32) * dp for p, dp in zip(ps, dps)]
        dss = [(pd - p.astype(F32) * jnp.sum(pd, axis=-1, keepdims=True)).astype(BF) for p, pd in zip(ps, pds)]
        for (f, h), g, p, ds in zip(some, gs, ps, dss):
            gq_s[at(f, h, 2)] = tm(p, g).astype(BF)
            gq_s[at(f, h, 0)] = (mm(ds, qkv_s[at(f, h, 1)]) * SCALE).astype(BF)
            gq_s[at(f, h, 1)] = (tm(ds, qkv_s[at(f, h, 0)]) * SCALE).astype(BF)
    gq = gq_s[...]
    n2 = mt(gq, wrq[...])
    dg2[...] += fold8(n2 * xhat2)
    db2[...] += fold8(n2)
    g_feat = g_row + norm_back(n2, xhat2, rstd2, g2[...])
    gf = g_feat.astype(BF)
    gaf_ref[...] = gf.reshape(FB, rows, D)
    arq[...] += tm(low2, gq)
    afo[...] += tm(h1, gf)
    h1_s[...] = mt(gf, wfo[...]).astype(BF)
    for k in range(n):
        for f in range(FB):
            for c, (r0, r1) in enumerate(spans):
                off = pl.multiple_of((me ^ k) * part + r0, 16)
                gh_refs[c * n + k][f] = h1_s[pl.ds(f * rows + off, r1 - r0), :]

    @pl.when(i == pl.num_programs(0) - 1)
    def _():
        if not first:
            for j in range(2):
                pltpu.make_async_copy(carried[j], kept[j], asems.at[j]).wait()

        def put(ref, blocks, at, a):
            ref[blocks, at] = (a if first else a + ref[blocks, at].astype(F32)).astype(BF)

        core = core_ref[0]
        row = 0
        for acc in accs[:4]:
            for j in range(acc.shape[1] // D):
                for b in range(D // (2 * ROWS_P)):
                    for side, ref in ((core, kept[0]), (1 - core, kept[1])):
                        here = pl.multiple_of((2 * b + side) * ROWS_P, ROWS_P)
                        put(ref, b, slice(row, row + ROWS_P), acc[pl.ds(here, ROWS_P), j * D : (j + 1) * D])
                row += ROWS_P
        unit = jnp.where(lax.broadcasted_iota(jnp.int32, (D, D), 0) == lax.broadcasted_iota(jnp.int32, (D, D), 1), 1.0, 0.0)
        for j in range(FF // D):
            turned = mt(unit.astype(BF), aout[:, j * D : (j + 1) * D].astype(BF)).reshape(4, 2, 4 * ROWS_P, D)
            even, odd = turned[:, 0], turned[:, 1]
            blocks = slice(j * 4, (j + 1) * 4)
            put(kept[0], blocks, slice(row, None), jnp.where(core == 0, even, odd))
            put(kept[1], blocks, slice(row, None), jnp.where(core == 0, odd, even))


def middle(me, core, x, hs, cot, bias, pack, g2, b2, g3, b3, f0, spans, carried):
    n = len(hs)
    _, feats, rows, _ = x.shape
    part = rows // n
    m = FB * rows
    count = hs[0].shape[0]
    first = not carried
    any_ = pl.BlockSpec(memory_space=pl.ANY)
    xblk = pl.BlockSpec((1, FB, rows, D), lambda i, *_: (0, i + f0 // FB, 0, 0))
    hblk = lambda r: pl.BlockSpec((FB, r, D), lambda i, *_: (i, 0, 0))
    sds = jax.ShapeDtypeStruct
    sums = [(D, D), (D, QKV), (D, D), (D, FF), (D, FF)]
    halves = [(pack.shape[0] // 2,) + pack.shape[1:]] * 2
    kept_specs = [pl.BlockSpec(q, lambda i, *_: (0, 0, 0)) for q in halves]
    kept_shape = [sds(q, BF) for q in halves]
    args = [x, *hs, cot, bias, pack, g2, b2, g3, b3, *carried]
    return pl.pallas_call(
        lambda *r: middle_kernel(*r, n=n, rows=rows, part=part, spans=spans, first=first),
        grid_spec=pltpu.PrefetchScalarGridSpec(
            num_scalar_prefetch=2,
            grid=(count // FB,),
            in_specs=[xblk]
            + [hblk(part)] * n
            + [xblk, full((rows, rows)), any_, full((1, D)), full((1, D)), full((1, D)), full((1, D))]
            + ([] if first else [any_] * 2 + [full((8, D))] * 4 + [any_] * 2),
            out_specs=[xblk, pl.BlockSpec((FB, rows, D), lambda i, *_: (i + f0 // FB, 0, 0))]
            + [hblk(r1 - r0) for r0, r1 in spans for _ in range(n)]
            + kept_specs
            + [pl.BlockSpec((8, D), lambda i, *_: (0, 0))] * 4,
            scratch_shapes=[
                pltpu.VMEM((m, D), BF),
                pltpu.VMEM((m, QKV), BF),
                pltpu.VMEM((FB * HEADS, rows, rows), BF),
                pltpu.VMEM((m, QKV), BF),
                pltpu.VMEM((m, D), BF),
                pltpu.VMEM((m, D), BF),
            ]
            + [pltpu.VMEM(q, F32) for q in sums]
            + [
                pltpu.VMEM((32, ROWS_P, D), BF),
                pltpu.VMEM((32, ROWS_P, QKV), BF),
                pltpu.VMEM((32, ROWS_P, D), BF),
                pltpu.VMEM((32, ROWS_P, FF), BF),
                pltpu.VMEM((32, 4 * ROWS_P, D), BF),
                pltpu.SemaphoreType.DMA((10,)),
                pltpu.SemaphoreType.DMA((2,)),
            ],
        ),
        out_shape=[sds(x.shape, BF), sds((feats, rows, D), BF)]
        + [sds((count, r1 - r0, D), BF) for r0, r1 in spans for _ in range(n)]
        + kept_shape
        + [sds((8, D), F32)] * 4,
        input_output_aliases={} if first else {2 + len(args) - 2: 0, 2 + len(args) - 1: 1},
        compiler_params=pltpu.CompilerParams(vmem_limit_bytes=VMEM),
        cost_estimate=COST,
        name="middle",
    )(me, core, *args)


def final_kernel(me_ref, g_ref, *refs, n):
    out = refs[-1]
    for k in range(n):
        at = pl.ds(me_ref[0] ^ k, 1)
        out[0, :, at, 0] = g_ref[:, at, 0].astype(F32) + refs[k][...][:, None].astype(F32)


def final(me, g, ds, r0, before):
    n = len(ds)
    feats, rows, _ = g.shape
    count = ds[0].shape[1]
    each = rows // n // count
    fb = next(q for q in (4, 3, 2, 1) if feats % q == 0)
    more = [] if before is None else [before.reshape(1, feats, n, each, count, D)]
    out = pl.pallas_call(
        lambda *r: final_kernel(*r, n=n),
        grid_spec=pltpu.PrefetchScalarGridSpec(
            num_scalar_prefetch=1,
            grid=(feats // fb,),
            in_specs=[pl.BlockSpec((fb, n, 1, count, D), lambda i, me: (i, 0, r0 // count, 0, 0))]
            + [pl.BlockSpec((fb, count, D), lambda i, me: (i, 0, 0))] * n
            + [pl.BlockSpec(memory_space=pl.ANY)] * len(more),
            out_specs=pl.BlockSpec((1, fb, n, 1, count, D), lambda i, me: (0, i, 0, r0 // count, 0, 0)),
        ),
        out_shape=jax.ShapeDtypeStruct((1, feats, n, each, count, D), F32),
        input_output_aliases={2 + n: 0} if more else {},
        compiler_params=pltpu.CompilerParams(vmem_limit_bytes=VMEM),
        cost_estimate=COST,
        name="final",
    )(me, g.reshape(feats, n, each, count, D), *ds, *more)
    return out.reshape(1, feats, rows, D)


def pack_kernel(*refs):
    vectors, qkv, *mats, down, first, pack = refs
    first[:, :QKV] = qkv[...]
    r = qkv.shape[0]
    first[:, QKV:] = jnp.broadcast_to(vectors[...], (r, 128))
    at = 0
    for m in mats:
        for j in range(m.shape[1] // D):
            pack[at : at + r] = m[:, j * D : (j + 1) * D]
            at += r
    pack[at:] = down[...]


def pack_shards(vectors, qkv, mats, down):
    r = qkv.shape[0]
    if r % ROWS_P:
        pack = jnp.concatenate([m[:, j * D : (j + 1) * D] for m in mats for j in range(m.shape[1] // D)] + [down], axis=0)
        return jnp.concatenate([qkv, jnp.broadcast_to(vectors, (r, 128))], axis=1), pack
    return pl.pallas_call(
        pack_kernel, out_shape=[jax.ShapeDtypeStruct((r, QKV + 128), BF), jax.ShapeDtypeStruct((13 * r, D), BF)], name="pack"
    )(vectors, qkv, *mats, down)


def row_allowed(segments, context):
    tables = jnp.arange(context.shape[0], dtype=jnp.int32)
    member = (segments[:, None] == tables[None, :]).astype(jnp.int32)
    sizes = jnp.sum(member, axis=0)
    starts = jnp.cumsum(sizes) - sizes
    places = jnp.arange(segments.shape[0], dtype=jnp.int32) - jnp.sum(member * starts[None, :], axis=1)
    limits = jnp.sum(member * context[None, :], axis=1)
    usable = places < limits
    return (segments[:, None] == segments[None, :]) & usable[None, :]


def swap(arrays, n):
    return [arrays[0]] + [lax.ppermute(arrays[k], "feat", [(d, d ^ k) for d in range(n)]) for k in range(1, n)]


def exchange(x, me, n):
    feats, rows, _ = x.shape

    def move(a, at, rows, bit):
        low = ((me // bit) % 2) * rows
        sent = lax.dynamic_slice(a, (0, at + rows - low, 0), (feats, rows, D))
        return lax.ppermute(sent, "feat", [(d, d ^ bit) for d in range(n)]), at + low

    bit = n // 2
    got, low = move(x, 0, rows // 2, bit)
    got = [got]

    def finish():
        have, places, half, bit = [(x, low), (got[0], 0)], [0, n // 2], rows // 2, n // 4
        while bit:
            half //= 2
            moved = [move(a, at, half, bit) for a, at in have]
            have = [(a, at) for (a, _), (_, at) in zip(have, moved)] + [(a, 0) for a, _ in moved]
            places = places + [q ^ bit for q in places]
            bit //= 2
        return [have[places.index(k)] for k in range(n)]

    return got, finish


class Shards:
    def __init__(self, rows, n):
        self.count = rows * n
        self.bits = [("rows", 1 << b) for b in reversed(range(rows.bit_length() - 1))]
        self.bits += [("feat", 1 << b) for b in reversed(range(n.bit_length() - 1))]
        self.sizes = {"rows": rows, "feat": n}
        last = len(self.bits) - 1
        self.rows_bits = list(range(rows.bit_length() - 1))
        self.near = last
        self.feat_bits = list(range(rows.bit_length() - 1, last))

    def other(self, a, at):
        axis, bit = self.bits[at]
        return lax.ppermute(a, axis, [(d, d ^ bit) for d in range(self.sizes[axis])])

    def side(self, at):
        axis, bit = self.bits[at]
        return (lax.axis_index(axis) // bit) % 2

    def gather(self, a, order):
        if a.ndim == 2:
            a = a.reshape((1,) * len(self.bits) + a.shape)
        while order:
            at, *rest = order
            if rest and rest[0] == at + 1 and self.bits[at][0] == "rows" == self.bits[at + 1][0] and self.sizes["rows"] <= 8:
                a = self.gather_two(a, at)
                order = rest[1:]
                continue
            b = self.other(a, at)
            low = self.side(at) == 0
            a = jnp.concatenate([jnp.where(low, a, b), jnp.where(low, b, a)], axis=at)
            order = rest
        return a

    def gather_two(self, a, at):
        axis, high = self.bits[at]
        low = self.bits[at + 1][1]
        move = lambda mask: lax.ppermute(a, axis, [(d, d ^ mask) for d in range(self.sizes[axis])])
        all_ = [[a, move(low)], [move(high), move(high | low)]]
        line = lambda q, side: jnp.concatenate([jnp.where(side, q[1], q[0]), jnp.where(side, q[0], q[1])], axis=at + 1)
        q = [line(pair, self.side(at + 1) == 1) for pair in all_]
        side = self.side(at) == 1
        return jnp.concatenate([jnp.where(side, q[1], q[0]), jnp.where(side, q[0], q[1])], axis=at)

    def halve(self, a, at):
        side = self.side(at)
        return [lax.dynamic_index_in_dim(a, i, at, True) for i in (side, 1 - side)]

    def quarter(self, a, at):
        high, low = self.side(at), self.side(at + 1)
        pick = lambda i, j: lax.dynamic_index_in_dim(lax.dynamic_index_in_dim(a, i, at, True), j, at + 1, True)
        return pick(high, low), [pick(high, 1 - low), pick(1 - high, low), pick(1 - high, 1 - low)]

    def others(self, parts, at):
        axis, high = self.bits[at]
        low = self.bits[at + 1][1]
        masks = (low, high, high | low)
        return [lax.ppermute(a, axis, [(d, d ^ mask) for d in range(self.sizes[axis])]) for a, mask in zip(parts, masks)]


def total(terms, held=BF):
    return sum([a.astype(F32) for a in terms[1:]], terms[0].astype(F32)).astype(held)


def begin(shards, sums, ats):
    halves = [shards.halve(a, at) for a, at in zip(sums, ats)]
    return [[mine, shards.other(others, at)] for (mine, others), at in zip(halves, ats)]


def unpack_kernel(*refs, counts):
    na, nb, nc = counts
    ins, outs = refs[: na + nb + nc], refs[na + nb + nc :]
    add = lambda terms, rows, cols=slice(None): sum([t[rows, cols].astype(F32) for t in terms[1:]], terms[0][rows, cols].astype(F32))
    a, b, c = ins[:na], ins[na : na + nb], ins[na + nb :]
    out_one, qkv_two, out_two, up, down, qkv_one, vectors = outs
    r = out_one.shape[0]
    at = 0
    for ref in (out_one, qkv_two, out_two, up):
        for j in range(ref.shape[1] // D):
            terms, row = (a, at) if at < SHARE else (b, at - SHARE)
            ref[:, j * D : (j + 1) * D] = add(terms, slice(row, row + r))
            at += r
    down[...] = add(b, slice(at - SHARE, at - SHARE + down.shape[0]))
    qkv_one[...] = add(c, slice(None), slice(0, QKV))
    vectors[...] = add(c, slice(None), slice(QKV, QKV + 128)).T


def unpack(two, dfirst, r):
    sums = [[a.reshape(a.shape[-2:]) for a in terms] for terms in (*two, dfirst)]
    if r % ROWS_P:
        pack = jnp.concatenate([total(sums[0], F32), total(sums[1], F32)])
        piece = lambda a, b: jnp.concatenate([pack[j * r : (j + 1) * r] for j in range(a, b)], axis=1)
        dfirst = total(sums[2], F32)
        return piece(0, 1), piece(1, 4), piece(4, 5), piece(5, 9), pack[9 * r :], dfirst[:, :QKV], dfirst[:, QKV:].T
    shapes = [(r, D), (r, QKV), (r, D), (r, FF), (4 * r, D), (r, QKV), (128, r)]
    return pl.pallas_call(
        lambda *refs: unpack_kernel(*refs, counts=[len(terms) for terms in sums]),
        out_shape=[jax.ShapeDtypeStruct(q, F32) for q in shapes],
        name="unpack",
    )(*[a for terms in sums for a in terms])


def split_sum(shards, mine, others, core):
    if shards.count == D // ROWS_P:
        terms = [mine, shards.other(others, shards.near)]
        return [a.reshape((2,) * (len(shards.bits) - 1) + (1,) + a.shape[1:]) for a in terms]
    both = jnp.where(core == 0, jnp.stack((mine, others), 1), jnp.stack((others, mine), 1))
    both = both.reshape((D // ROWS_P,) + mine.shape[1:])
    if mine.shape[1] == ROWS_P:
        both = both.reshape(shards.count, -1, both.shape[2])
    else:
        both = repack(both, shards.count)
    return begin(shards, [both.reshape((2,) * len(shards.bits) + both.shape[1:])], [shards.near])[0]


def together(a, b):
    return lax.optimization_barrier((a, b))


def repack(a, blocks):
    count = a.shape[0]
    if count == blocks:
        return a
    r, q = D // count, D // blocks
    parts = [a[:, j * r : (j + 1) * r].reshape(blocks, q, D) for j in range(9)]
    return jnp.concatenate(parts + [a[:, 9 * r :].reshape(blocks, 4 * q, D)], axis=1)


def per_device(rows_axis, n, inputs, *rest):
    weights, (cotangent, segments, context, feature_mask) = rest[:12], rest[12:]
    gain_one, shift_one, qkv_one, out_one, gain_two, shift_two, qkv_two, out_two, gain_three, shift_three, up, down = weights
    shards = Shards(rows_axis, n)
    _, feats, rows, _ = inputs.shape
    part = rows // n
    tot = n * feats
    me = lax.axis_index("feat").astype(jnp.int32)
    me_arr = me.reshape(1)

    core = (me % 2).reshape(1)
    vectors = (gain_one, shift_one, gain_two, shift_two, gain_three, shift_three)
    r = D // shards.count
    vectors = sum(jnp.pad(v, (j * r, 128 - (j + 1) * r)) for j, v in enumerate(vectors)).reshape(1, 128)
    first, pack = pack_shards(vectors, qkv_one, (out_one, qkv_two, out_two, up), down)
    pack = repack(lax.all_gather(pack, ("rows", "feat"), axis=0), D // ROWS_P)
    first = shards.gather(first, shards.feat_bits[:1])
    got, xs_at = exchange(together(inputs, first)[0][0], me, n)
    first = shards.gather(first, shards.feat_bits[1:] + shards.rows_bits)
    got[0], first = together(got[0], first)
    xs_at = xs_at()
    first = shards.gather(first, [shards.near]).reshape(D, QKV + 128)
    gains = first.reshape(shards.count, r, QKV + 128)[:, 0, QKV : QKV + 6 * r].reshape(shards.count, 6, r)
    gains = gains.transpose(1, 0, 2).reshape(6, D).astype(F32)
    g1, b1, g2, b2, g3, b3 = [gains[j : j + 1] for j in range(6)]

    xs = [a for a, _ in xs_at]
    x_rows = jnp.stack([jnp.asarray(at, jnp.int32) // RC for _, at in xs_at] + [core[0]])
    order = me ^ jnp.arange(n, dtype=jnp.int32)
    valid = jnp.take(feature_mask[0].reshape(n, feats), order, axis=0).reshape(tot) > 0
    wide = -(-2 * tot // 128) * 128
    lane = jnp.arange(wide)
    same = (lane[None, :] // tot == jnp.arange(2 * tot)[:, None] // tot) & (lane < 2 * tot)[None, :]
    bias_one = jnp.where(same & jnp.pad(jnp.tile(valid, 2), (0, wide - 2 * tot))[None, :], 0.0, MASKED).astype(F32)
    bias_two = jnp.where(row_allowed(segments[0], context[0]), 0.0, MASKED).astype(F32)

    cut = feats // 3 // FB * FB
    cuts = ((0, cut), (cut, feats))
    half = part // 2
    res = feature_forward(x_rows, xs, g1, b1, first, bias_one, cuts, part)
    qkv, p = res[2 * n :]
    h_a, h_b = swap(res[:n], n), swap(res[n : 2 * n], n)
    gains_two = (g2, b2, g3, b3)
    res = middle(me_arr, core, inputs, h_a, cotangent, bias_two, pack, *gains_two, 0, ((0, part),), [])
    output, gaf, carried = res[0], res[1], res[2 + n :]
    g_a = swap(res[2 : 2 + n], n)
    spans = ((0, half), (half, part))
    res = middle(me_arr, core, inputs, h_b, cotangent, bias_two, pack, *gains_two, cut, spans, [*carried, output, gaf])
    g_a, res = together(g_a, res)
    output, gaf = res[:2]
    g_b, g_c = swap(res[2 : 2 + n], n), swap(res[2 + n : 2 + 2 * n], n)
    mine, others, *vector_grads = res[2 + 2 * n :]

    wide_first, tall_first = shards.rows_bits[::-1], shards.rows_bits[-2::-1] + shards.rows_bits[-1:]
    ways = [way + shards.feat_bits for way in (wide_first, tall_first)]
    on = lambda i: [way[i] for way in ways]
    dpack = total(split_sum(shards, mine, others, core[0]))
    dpack, g_b = together(dpack, g_b)
    share = SHARE if shards.count == D // ROWS_P else dpack.shape[-2] // 2
    two = [dpack[..., :share, :], dpack[..., share:, :]]

    two = begin(shards, two, on(0))
    *d_a, acc, dg1, db1 = feature_backward(
        x_rows, xs, [(0, g_a), (0, g_b)], qkv, p, g1, b1, first, cuts, 0, half, [], []
    )
    two, d_a, g_c = lax.optimization_barrier((two, d_a, g_c))
    two, g_c = together([total(terms) for terms in two], g_c)

    two = begin(shards, two, on(1))
    d_a = swap(d_a, n)
    *d_b, kept, others = feature_backward(
        x_rows, xs, [(0, g_a), (half, g_c)], qkv, p, g1, b1, first, cuts, half, part, [acc, dg1, db1], vector_grads
    )
    two, d_a, d_b, kept, others = lax.optimization_barrier((two, d_a, d_b, kept, others))
    dfirst = total(split_sum(shards, kept, others, core[0]))
    d_b = swap(d_b, n)
    two = [total(terms) for terms in two]
    for i in range(2, len(ways[0]) - 2):
        two = [total(terms) for terms in begin(shards, two, on(i))]
    d_a, dfirst = together(d_a, dfirst)

    *two, dfirst = begin(shards, [*two, dfirst], on(-2) + wide_first[:1])
    input_grad = final(me_arr, gaf, d_a, 0, None)
    two, dfirst, input_grad = lax.optimization_barrier((two, dfirst, input_grad))
    two = begin(shards, [total(terms) for terms in two], on(-1))
    dfirst = total(dfirst)
    last = wide_first[1:] + shards.feat_bits
    if len(last) == 3:
        kept, others = shards.quarter(dfirst, last[1])
        two, others, d_b = lax.optimization_barrier((two, shards.others(others, last[1]), d_b))
        input_grad = final(me_arr, gaf, d_b, half, input_grad)
        two, others, input_grad = lax.optimization_barrier((two, others, input_grad))
        dfirst = total([kept] + others)
        last = last[2:]
    else:
        input_grad = final(me_arr, gaf, d_b, half, input_grad)
    for at in last[:-1]:
        dfirst = total(begin(shards, [dfirst], [at])[0])
    dfirst = begin(shards, [dfirst], last[-1:])[0]
    d_out_one, d_qkv_two, d_out_two, d_up, d_down, d_qkv_one, vectors = unpack(two, dfirst, r)
    v = [vectors[j] for j in range(6)]
    return (output, input_grad, v[0], v[1], d_qkv_one, d_out_one, v[2], v[3], d_qkv_two, d_out_two, v[4], v[5], d_up, d_down)


def solution(mesh):
    rows_axis, n = mesh.shape["rows"], mesh.shape["feat"]
    vec, mat, act, tab = P(("rows", "feat")), P(("rows", "feat"), None), P("rows", "feat", None, None), P("rows", None)
    weights = (vec, vec, mat, mat, vec, vec, mat, mat, vec, vec, mat, mat)
    return jax.shard_map(
        lambda *a: per_device(rows_axis, n, *a),
        mesh=mesh,
        in_specs=(act,) + weights + (act, tab, tab, tab),
        out_specs=(act, act) + weights,
        check_vma=False,
    )
```

```python
import math

import jax
import jax.numpy as jnp
import numpy as np
from jax import lax
from jax.experimental import pallas as pl
from jax.experimental.pallas import tpu as pltpu
from jax.sharding import PartitionSpec as P

D = 512
HEADS = 4
HEAD_DIM = 128
FF = 2048
QKV = 3 * D
EPS = 1e-05
MASKED = -1e30
SCALE = HEAD_DIM**-0.5
BF = jnp.bfloat16
F32 = jnp.float32
LOG2E = float(np.log2(np.e))
VMEM = 60 * 1024 * 1024

GRP2 = 8
GRP = 8
SHARE = 112
ROWS_P = 16
COST = pl.CostEstimate(flops=10**11, bytes_accessed=10**6, transcendentals=0)
RC = 16
FCH = 256
FB = 2


def mm(a, b):
    return lax.dot_general(a, b, (((1,), (0,)), ((), ())), preferred_element_type=F32)


def mt(a, b):
    return lax.dot_general(a, b, (((1,), (1,)), ((), ())), preferred_element_type=F32)


def tm(a, b):
    return lax.dot_general(a, b, (((0,), (0,)), ((), ())), preferred_element_type=F32)


def norm(x):
    mean = jnp.mean(x, axis=-1, keepdims=True)
    centred = x - mean
    var = jnp.mean(centred * centred, axis=-1, keepdims=True)
    rstd = lax.rsqrt(var + EPS)
    return centred * rstd, rstd


def norm_back(n, xhat, rstd, gain):
    e = n * gain
    m1 = jnp.mean(e, axis=-1, keepdims=True)
    m2 = jnp.mean(e * xhat, axis=-1, keepdims=True)
    return rstd * (e - m1 - xhat * m2)


def fold8(a):
    return jnp.sum(a.reshape(a.shape[0] // 8, 8, a.shape[1]), axis=0)


def gelu_pair(h):
    e = jnp.exp2(h * h * (-0.5 * LOG2E))
    d = 1.0 + (0.3275911 * 2**-0.5) * jnp.abs(h)
    t = pl.reciprocal(d, approx=True)
    t = t * (2.0 - d * t)
    poly = 0.5 * 1.061405429
    for c in (-1.453152027, 1.421413741, -0.284496736, 0.254829592):
        poly = poly * t + 0.5 * c
    q = poly * t * e
    cdf = jnp.where(h >= 0, 1.0 - q, q)
    return h * cdf, cdf + h * e * (2 * np.pi) ** -0.5


def by_rows(parts):
    a = jnp.swapaxes(jnp.concatenate(parts, axis=0), 0, 1)
    return a.reshape(a.shape[0] * a.shape[1], D)


def by_features(a, tot):
    return jnp.swapaxes(a.reshape(a.shape[0] // tot, tot, D), 0, 1)


def full(shape):
    return pl.BlockSpec(shape, lambda *_: (0,) * len(shape), pipeline_mode=pl.Buffered(1))


def feature_forward_kernel(_, *refs, n, feats, cuts):
    x_refs, (gain, shift, wqkv, bias), outs = refs[:n], refs[n : n + 4], refs[n + 4 :]
    nc = n * len(cuts)
    h_refs, (qkv_ref, p_ref), (xs, low, hs) = outs[:nc], outs[nc : nc + 2], outs[nc + 2 :]
    tot = n * feats
    pair = 2 * tot
    wide = bias.shape[1]
    xs[...] = by_rows([x_refs[k][...] for k in range(n)])
    for r in range(RC):
        at = slice(r * tot, (r + 1) * tot)
        xhat, _ = norm(xs[at].astype(F32))
        low[at] = (xhat * gain[...] + shift[...]).astype(BF)
    rows = tot * RC
    qkv_ref[0, :rows] = mm(low[...], wqkv[...]).astype(BF)
    qkv_ref[0, rows:] = jnp.zeros((qkv_ref.shape[1] - rows, QKV), BF)
    mask = bias[...]
    for b0 in range(0, RC // 2, GRP):
        jobs = [(b, h) for b in range(b0, b0 + GRP) for h in range(HEADS)]
        at = lambda b, h, c, w: (0, slice(b * pair, b * pair + w), slice(c * D + h * 128, c * D + h * 128 + 128))
        ss = [mt(qkv_ref[at(b, h, 0, pair)], qkv_ref[at(b, h, 1, wide)]) * (SCALE * LOG2E) + mask for b, h in jobs]
        es = [jnp.exp2(s - jnp.max(s, axis=-1, keepdims=True)) for s in ss]
        ps = [(e * (1.0 / jnp.sum(e, axis=-1, keepdims=True))).astype(BF) for e in es]
        os = [mm(p, qkv_ref[at(b, h, 2, wide)]) for p, (b, h) in zip(ps, jobs)]
        for p, o, (b, h) in zip(ps, os, jobs):
            p_ref[0, b, h] = p
            hs[b * pair : (b + 1) * pair, h * 128 : h * 128 + 128] = o.astype(BF)
    heads = by_features(hs[...], tot)
    for c, (f0, f1) in enumerate(cuts):
        for k in range(n):
            h_refs[c * n + k][...] = heads[k * feats + f0 : k * feats + f1]


def feature_forward(x_rows, xs, gain, shift, wqkv, bias, cuts, rows):
    n = len(xs)
    feats = xs[0].shape[0]
    tot = n * feats
    steps = rows // RC
    pad = tot * RC - 2 * tot + bias.shape[1]
    sds = jax.ShapeDtypeStruct
    return pl.pallas_call(
        lambda *r: feature_forward_kernel(*r, n=n, feats=feats, cuts=cuts),
        grid_spec=pltpu.PrefetchScalarGridSpec(
            num_scalar_prefetch=1,
            grid=(steps,),
            in_specs=[pl.BlockSpec((feats, RC, D), lambda i, at, k=k: (0, i + at[k], 0)) for k in range(n)]
            + [full((1, D)), full((1, D)), full((D, QKV)), full(bias.shape)],
            out_specs=[pl.BlockSpec((f1 - f0, RC, D), lambda i, at: (0, i, 0)) for f0, f1 in cuts for _ in range(n)]
            + [
                pl.BlockSpec((1, pad, QKV), lambda i, at: (i, 0, 0)),
                pl.BlockSpec((1, RC // 2, HEADS, 2 * tot, bias.shape[1]), lambda i, at: (i, 0, 0, 0, 0)),
            ],
            scratch_shapes=[
                pltpu.VMEM((tot * RC, D), BF),
                pltpu.VMEM((tot * RC, D), BF),
                pltpu.VMEM((tot * RC, D), BF),
            ],
        ),
        out_shape=[sds((f1 - f0, rows, D), BF) for f0, f1 in cuts for _ in range(n)]
        + [sds((steps, pad, QKV), BF), sds((steps, RC // 2, HEADS, 2 * tot, bias.shape[1]), BF)],
        compiler_params=pltpu.CompilerParams(vmem_limit_bytes=VMEM),
        cost_estimate=COST,
        name="feature_forward",
    )(x_rows, *xs, gain, shift, wqkv, bias)


def feature_backward_kernel(at_ref, *refs, n, feats, cuts, first, last):
    it = iter(refs)
    take = lambda c: [next(it) for _ in range(c)]
    x_refs = take(n)
    g_refs = take(n * len(cuts))
    qkv_ref, p_ref, gain, shift, wqkv = take(5)
    carried = [] if first else take(3)
    others = take(4) if last else []
    d_refs = take(n)
    outs = take(2) if last else take(3)
    dgain, dshift, vecs, xs, xh, rs, ns, low, gh, gqkv, acc = take(11)
    if not last:
        acc, dgain, dshift = outs
    tot = n * feats
    pair = 2 * tot
    wide = p_ref.shape[-1]
    i = pl.program_id(0)

    @pl.when(i == 0)
    def _():
        for j, a in enumerate((acc, dgain, dshift)):
            a[...] = jnp.zeros_like(a) if first else carried[j][...]

    xs[...] = by_rows([x_refs[k][...] for k in range(n)])
    gh[...] = by_rows([g_refs[c * n + k][...] for k in range(n) for c in range(len(cuts))])
    for r in range(RC):
        at = slice(r * tot, (r + 1) * tot)
        xhat, rstd = norm(xs[at].astype(F32))
        xh[at] = xhat
        rs[at] = jnp.broadcast_to(rstd, (tot, 128))
        low[at] = (xhat * gain[...] + shift[...]).astype(BF)
    for b0 in range(0, RC // 2, GRP):
        jobs = [(b, h) for b in range(b0, b0 + GRP) for h in range(HEADS)]
        at = lambda b, h, c, w: (0, slice(b * pair, b * pair + w), slice(c * D + h * 128, c * D + h * 128 + 128))
        gs_ = [gh[b * pair : (b + 1) * pair, h * 128 : h * 128 + 128] for b, h in jobs]
        dps = [mt(g, qkv_ref[at(b, h, 2, wide)]) for g, (b, h) in zip(gs_, jobs)]
        ps = [p_ref[0, b, h] for b, h in jobs]
        dvs = [tm(p, g) for p, g in zip(ps, gs_)]
        pds = [p.astype(F32) * dp for p, dp in zip(ps, dps)]
        dss = [(pd - p.astype(F32) * jnp.sum(pd, axis=-1, keepdims=True)).astype(BF) for p, pd in zip(ps, pds)]
        dqs = [mm(ds, qkv_ref[at(b, h, 1, wide)]) for ds, (b, h) in zip(dss, jobs)]
        dks = [tm(ds, qkv_ref[at(b, h, 0, pair)]) for ds, (b, h) in zip(dss, jobs)]
        for (b, h), dq, dk, dv in zip(jobs, dqs, dks, dvs):
            span = slice(b * pair, (b + 1) * pair)
            gqkv[span, h * 128 : h * 128 + 128] = (dq * SCALE).astype(BF)
            gqkv[span, D + h * 128 : D + h * 128 + 128] = (dk * SCALE).astype(BF)[:pair]
            gqkv[span, 2 * D + h * 128 : 2 * D + h * 128 + 128] = dv.astype(BF)[:pair]
    acc[...] += tm(low[...], gqkv[...])
    ns[...] = mt(gqkv[...], wqkv[...])
    for r in range(RC):
        at = slice(r * tot, (r + 1) * tot)
        xhat = xh[at]
        nn = ns[at]
        dgain[...] += fold8(nn * xhat)
        dshift[...] += fold8(nn)
        xs[at] = norm_back(nn, xhat, rs[at, :1], gain[...]).astype(BF)
    back = by_features(xs[...], tot)
    for k in range(n):
        d_refs[k][...] = back[k * feats : (k + 1) * feats]

    if last:

        @pl.when(i == pl.num_programs(0) - 1)
        def _():
            core = at_ref[n]
            vecs[...] = jnp.zeros_like(vecs)
            for j, v in enumerate([dgain, dshift] + others):
                vecs[j : j + 1] = jnp.sum(v[...], axis=0, keepdims=True)
            turned = vecs[...].T.astype(BF).reshape(D // (2 * ROWS_P), 2, ROWS_P, 128)
            outs[0][:, :, QKV:] = jnp.where(core == 0, turned[:, 0], turned[:, 1])
            outs[1][:, :, QKV:] = jnp.where(core == 0, turned[:, 1], turned[:, 0])
            for b in range(D // (2 * ROWS_P)):
                for side, ref in ((core, outs[0]), (1 - core, outs[1])):
                    row = pl.multiple_of((2 * b + side) * ROWS_P, ROWS_P)
                    ref[b, :, :QKV] = acc[pl.ds(row, ROWS_P), :].astype(BF)


def feature_backward(x_rows, xs, gs, qkv, p, gain, shift, wqkv, cuts, r0, r1, carried, others):
    n = len(xs)
    feats = xs[0].shape[0]
    tot = n * feats
    s0, steps = r0 // RC, (r1 - r0) // RC
    first, last = not carried, bool(others)
    sds = jax.ShapeDtypeStruct
    at = lambda f, row: pl.BlockSpec((f, RC, D), lambda i, _: (0, i + (r0 - row) // RC, 0))
    sums = [(D, QKV), (8, D), (8, D)]
    if last:
        each = (D // (2 * ROWS_P), ROWS_P, QKV + 128)
        out_specs, out_shape = [pl.BlockSpec(each, lambda i, _: (0, 0, 0))] * 2, [sds(each, BF)] * 2
    else:
        out_specs, out_shape = [pl.BlockSpec(q, lambda i, _: (0, 0)) for q in sums], [sds(q, F32) for q in sums]
    return pl.pallas_call(
        lambda *r: feature_backward_kernel(*r, n=n, feats=feats, cuts=cuts, first=first, last=last),
        grid_spec=pltpu.PrefetchScalarGridSpec(
            num_scalar_prefetch=1,
            grid=(steps,),
            in_specs=[pl.BlockSpec((feats, RC, D), lambda i, q, k=k: (0, i + s0 + q[k], 0)) for k in range(n)]
            + [at(f1 - f0, row) for (f0, f1), (row, _) in zip(cuts, gs) for _ in range(n)]
            + [
                pl.BlockSpec((1,) + qkv.shape[1:], lambda i, _: (i + s0, 0, 0)),
                pl.BlockSpec((1,) + p.shape[1:], lambda i, _: (i + s0, 0, 0, 0, 0)),
                full((1, D)),
                full((1, D)),
                full((D, QKV)),
            ]
            + [full(q.shape) for q in carried]
            + [full((8, D)) for _ in others],
            out_specs=[at(feats, r0)] * n + out_specs,
            scratch_shapes=[
                pltpu.VMEM((8, D), F32),
                pltpu.VMEM((8, D), F32),
                pltpu.VMEM((128, D), F32),
                pltpu.VMEM((tot * RC, D), BF),
                pltpu.VMEM((tot * RC, D), F32),
                pltpu.VMEM((tot * RC, 128), F32),
                pltpu.VMEM((tot * RC, D), F32),
                pltpu.VMEM((tot * RC, D), BF),
                pltpu.VMEM((tot * RC, D), BF),
                pltpu.VMEM((tot * RC, QKV), BF),
                pltpu.VMEM((D, QKV), F32),
            ],
        ),
        out_shape=[sds((feats, r1 - r0, D), BF)] * n + out_shape,
        compiler_params=pltpu.CompilerParams(vmem_limit_bytes=VMEM),
        cost_estimate=COST,
        name="feature_backward",
    )(x_rows, *xs, *[a for _, part in gs for a in part], qkv, p, gain, shift, wqkv, *carried, *others)


class Flat:
    def __init__(self, ref):
        self.ref = ref

    def __getitem__(self, key):
        rows, cols = (slice(None), slice(None)) if key is Ellipsis else key
        r = self.ref.shape[1]
        if rows.start is not None:
            rows = slice(rows.start // r, rows.stop // r)
        w = self.ref[rows, :, cols]
        return w.reshape(w.shape[0] * w.shape[1], w.shape[2])


def unpack_copies(pack, weights, sems):
    copies, at = [], 0
    for w in weights:
        r = w.shape[1]
        for j in range(w.shape[2] // D):
            src = pack.at[:, pl.ds(at, r), :]
            copies.append(pltpu.make_async_copy(src, w.at[:, :, pl.ds(j * D, D)], sems.at[len(copies)]))
            at += r
    return copies


def middle_kernel(me_ref, core_ref, *refs, n, rows, part, spans, first):
    it = iter(refs)
    take = lambda c: [next(it) for _ in range(c)]
    (x_ref,) = take(1)
    h_refs = take(n)
    cot_ref, bias, pack, g2, b2, g3, b3 = take(7)
    carried = [] if first else take(6)
    _ = [] if first else take(2)
    out_ref, gaf_ref = take(2)
    gh_refs = take(n * len(spans))
    kept = take(2)
    dg2, db2, dg3, db3 = take(4)
    h1_s, qkv_s, p_s, gq_s, heads_s, gh2_s, afo, arq, aro, ain, aout, wfo_s, wrq_s, wro_s, win_s, wout_s, sems, asems = take(18)
    i = pl.program_id(0)
    me = me_ref[0]
    m = FB * rows
    accs = (afo, arq, aro, ain, aout)

    @pl.when(i == 0)
    def _():
        copies = unpack_copies(pack, (wfo_s, wrq_s, wro_s, win_s, wout_s), sems)
        for c in copies:
            c.start()
        for a in (afo, arq, aro, ain, aout):
            a[...] = jnp.zeros_like(a)
        for j, a in enumerate((dg2, db2, dg3, db3)):
            a[...] = jnp.zeros_like(a) if first else carried[2 + j][...]
        if not first:
            for j in range(2):
                pltpu.make_async_copy(carried[j], kept[j], asems.at[j]).start()

    def need(*which):
        @pl.when(i == 0)
        def _():
            at = 0
            for j, w in enumerate((wfo_s, wrq_s, wro_s, win_s, wout_s)):
                for _ in range(w.shape[2] // D):
                    if j in which:
                        pltpu.make_async_copy(pack.at[:, pl.ds(0, w.shape[1]), :], w.at[:, :, pl.ds(0, D)], sems.at[at]).wait()
                    at += 1

    wfo, wrq, wro, win, wout = (Flat(w) for w in (wfo_s, wrq_s, wro_s, win_s, wout_s))
    for k in range(n):
        off = pl.multiple_of((me ^ k) * part, part)
        for f in range(FB):
            h1_s[pl.ds(f * rows + off, part), :] = h_refs[k][f]
    x = x_ref[0].reshape(m, D).astype(F32)
    h1 = h1_s[...]
    need(0)
    after_feat = x + mm(h1, wfo[...])
    xhat2, rstd2 = norm(after_feat)
    low2 = (xhat2 * g2[...] + b2[...]).astype(BF)
    need(*((1, 2, 3, 4) if first else (1,)))
    qkv_s[...] = mm(low2, wrq[...]).astype(BF)
    mask = bias[...]
    jobs = [(f, h) for f in range(FB) for h in range(HEADS)]
    at = lambda f, h, c: (slice(f * rows, (f + 1) * rows), slice(c * D + h * 128, c * D + h * 128 + 128))
    for g0 in range(0, len(jobs), GRP2):
        some = jobs[g0 : g0 + GRP2]
        ss = [mt(qkv_s[at(f, h, 0)], qkv_s[at(f, h, 1)]) * (SCALE * LOG2E) + mask for f, h in some]
        es = [jnp.exp2(s - jnp.max(s, axis=-1, keepdims=True)) for s in ss]
        ps = [(e * (1.0 / jnp.sum(e, axis=-1, keepdims=True))).astype(BF) for e in es]
        for p, (f, h) in zip(ps, some):
            p_s[f * HEADS + h] = p
            heads_s[at(f, h, 0)] = mm(p, qkv_s[at(f, h, 2)]).astype(BF)
    heads = heads_s[...]
    if not first:
        need(2, 3, 4)
    after_row = after_feat + mm(heads, wro[...])
    xhat3, rstd3 = norm(after_row)
    low3 = (xhat3 * g3[...] + b3[...]).astype(BF)
    cot = cot_ref[0].reshape(m, D)
    out = after_row
    n3 = None
    chunks = [slice(j * FCH, (j + 1) * FCH) for j in range(FF // FCH)]
    hid = mm(low3, win[:, chunks[0]])
    gact = mt(cot, wout[chunks[0], :])
    waiting = None
    for j, cols in enumerate(chunks + [None]):
        if cols is not None:
            act, slope = gelu_pair(hid)
            act = act.astype(BF)
            ghid = (gact * slope).astype(BF)
            if j + 1 < len(chunks):
                hid = mm(low3, win[:, chunks[j + 1]])
                gact = mt(cot, wout[chunks[j + 1], :])
        if waiting is not None:
            a0, g0, c0 = waiting
            out = out + mm(a0, wout[c0, :])
            back = mt(g0, win[:, c0])
            n3 = back if n3 is None else n3 + back
            aout[:, c0] += tm(cot, a0)
            ain[:, c0] += tm(low3, g0)
        waiting = (act, ghid, cols)
    out_ref[0] = out.astype(BF).reshape(FB, rows, D)
    dg3[...] += fold8(n3 * xhat3)
    db3[...] += fold8(n3)
    g_row = cot.astype(F32) + norm_back(n3, xhat3, rstd3, g3[...])
    gb = g_row.astype(BF)
    gh2_s[...] = mt(gb, wro[...]).astype(BF)
    aro[...] += tm(heads, gb)
    for g0 in range(0, len(jobs), GRP2):
        some = jobs[g0 : g0 + GRP2]
        gs = [gh2_s[at(f, h, 0)] for f, h in some]
        ps = [p_s[f * HEADS + h] for f, h in some]
        dps = [mt(g, qkv_s[at(f, h, 2)]) for g, (f, h) in zip(gs, some)]
        pds = [p.astype(F32) * dp for p, dp in zip(ps, dps)]
        dss = [(pd - p.astype(F32) * jnp.sum(pd, axis=-1, keepdims=True)).astype(BF) for p, pd in zip(ps, pds)]
        for (f, h), g, p, ds in zip(some, gs, ps, dss):
            gq_s[at(f, h, 2)] = tm(p, g).astype(BF)
            gq_s[at(f, h, 0)] = (mm(ds, qkv_s[at(f, h, 1)]) * SCALE).astype(BF)
            gq_s[at(f, h, 1)] = (tm(ds, qkv_s[at(f, h, 0)]) * SCALE).astype(BF)
    gq = gq_s[...]
    n2 = mt(gq, wrq[...])
    dg2[...] += fold8(n2 * xhat2)
    db2[...] += fold8(n2)
    g_feat = g_row + norm_back(n2, xhat2, rstd2, g2[...])
    gf = g_feat.astype(BF)
    gaf_ref[...] = gf.reshape(FB, rows, D)
    arq[...] += tm(low2, gq)
    afo[...] += tm(h1, gf)
    h1_s[...] = mt(gf, wfo[...]).astype(BF)
    for k in range(n):
        for f in range(FB):
            for c, (r0, r1) in enumerate(spans):
                off = pl.multiple_of((me ^ k) * part + r0, 16)
                gh_refs[c * n + k][f] = h1_s[pl.ds(f * rows + off, r1 - r0), :]

    @pl.when(i == pl.num_programs(0) - 1)
    def _():
        if not first:
            for j in range(2):
                pltpu.make_async_copy(carried[j], kept[j], asems.at[j]).wait()

        def put(ref, blocks, at, a):
            ref[blocks, at] = (a if first else a + ref[blocks, at].astype(F32)).astype(BF)

        core = core_ref[0]
        row = 0
        for acc in accs[:4]:
            for j in range(acc.shape[1] // D):
                for b in range(D // (2 * ROWS_P)):
                    for side, ref in ((core, kept[0]), (1 - core, kept[1])):
                        here = pl.multiple_of((2 * b + side) * ROWS_P, ROWS_P)
                        put(ref, b, slice(row, row + ROWS_P), acc[pl.ds(here, ROWS_P), j * D : (j + 1) * D])
                row += ROWS_P
        unit = jnp.where(lax.broadcasted_iota(jnp.int32, (D, D), 0) == lax.broadcasted_iota(jnp.int32, (D, D), 1), 1.0, 0.0)
        for j in range(FF // D):
            turned = mt(unit.astype(BF), aout[:, j * D : (j + 1) * D].astype(BF)).reshape(4, 2, 4 * ROWS_P, D)
            even, odd = turned[:, 0], turned[:, 1]
            blocks = slice(j * 4, (j + 1) * 4)
            put(kept[0], blocks, slice(row, None), jnp.where(core == 0, even, odd))
            put(kept[1], blocks, slice(row, None), jnp.where(core == 0, odd, even))


def middle(me, core, x, hs, cot, bias, pack, g2, b2, g3, b3, f0, spans, carried):
    n = len(hs)
    _, feats, rows, _ = x.shape
    part = rows // n
    m = FB * rows
    count = hs[0].shape[0]
    first = not carried
    any_ = pl.BlockSpec(memory_space=pl.ANY)
    xblk = pl.BlockSpec((1, FB, rows, D), lambda i, *_: (0, i + f0 // FB, 0, 0))
    hblk = lambda r: pl.BlockSpec((FB, r, D), lambda i, *_: (i, 0, 0))
    sds = jax.ShapeDtypeStruct
    sums = [(D, D), (D, QKV), (D, D), (D, FF), (D, FF)]
    halves = [(pack.shape[0] // 2,) + pack.shape[1:]] * 2
    kept_specs = [pl.BlockSpec(q, lambda i, *_: (0, 0, 0)) for q in halves]
    kept_shape = [sds(q, BF) for q in halves]
    args = [x, *hs, cot, bias, pack, g2, b2, g3, b3, *carried]
    return pl.pallas_call(
        lambda *r: middle_kernel(*r, n=n, rows=rows, part=part, spans=spans, first=first),
        grid_spec=pltpu.PrefetchScalarGridSpec(
            num_scalar_prefetch=2,
            grid=(count // FB,),
            in_specs=[xblk]
            + [hblk(part)] * n
            + [xblk, full((rows, rows)), any_, full((1, D)), full((1, D)), full((1, D)), full((1, D))]
            + ([] if first else [any_] * 2 + [full((8, D))] * 4 + [any_] * 2),
            out_specs=[xblk, pl.BlockSpec((FB, rows, D), lambda i, *_: (i + f0 // FB, 0, 0))]
            + [hblk(r1 - r0) for r0, r1 in spans for _ in range(n)]
            + kept_specs
            + [pl.BlockSpec((8, D), lambda i, *_: (0, 0))] * 4,
            scratch_shapes=[
                pltpu.VMEM((m, D), BF),
                pltpu.VMEM((m, QKV), BF),
                pltpu.VMEM((FB * HEADS, rows, rows), BF),
                pltpu.VMEM((m, QKV), BF),
                pltpu.VMEM((m, D), BF),
                pltpu.VMEM((m, D), BF),
            ]
            + [pltpu.VMEM(q, F32) for q in sums]
            + [
                pltpu.VMEM((32, ROWS_P, D), BF),
                pltpu.VMEM((32, ROWS_P, QKV), BF),
                pltpu.VMEM((32, ROWS_P, D), BF),
                pltpu.VMEM((32, ROWS_P, FF), BF),
                pltpu.VMEM((32, 4 * ROWS_P, D), BF),
                pltpu.SemaphoreType.DMA((10,)),
                pltpu.SemaphoreType.DMA((2,)),
            ],
        ),
        out_shape=[sds(x.shape, BF), sds((feats, rows, D), BF)]
        + [sds((count, r1 - r0, D), BF) for r0, r1 in spans for _ in range(n)]
        + kept_shape
        + [sds((8, D), F32)] * 4,
        input_output_aliases={} if first else {2 + len(args) - 2: 0, 2 + len(args) - 1: 1},
        compiler_params=pltpu.CompilerParams(vmem_limit_bytes=VMEM),
        cost_estimate=COST,
        name="middle",
    )(me, core, *args)


def final_kernel(me_ref, g_ref, *refs, n):
    out = refs[-1]
    for k in range(n):
        at = pl.ds(me_ref[0] ^ k, 1)
        out[0, :, at, 0] = g_ref[:, at, 0].astype(F32) + refs[k][...][:, None].astype(F32)


def final(me, g, ds, r0, before):
    n = len(ds)
    feats, rows, _ = g.shape
    count = ds[0].shape[1]
    each = rows // n // count
    fb = next(q for q in (4, 3, 2, 1) if feats % q == 0)
    more = [] if before is None else [before.reshape(1, feats, n, each, count, D)]
    out = pl.pallas_call(
        lambda *r: final_kernel(*r, n=n),
        grid_spec=pltpu.PrefetchScalarGridSpec(
            num_scalar_prefetch=1,
            grid=(feats // fb,),
            in_specs=[pl.BlockSpec((fb, n, 1, count, D), lambda i, me: (i, 0, r0 // count, 0, 0))]
            + [pl.BlockSpec((fb, count, D), lambda i, me: (i, 0, 0))] * n
            + [pl.BlockSpec(memory_space=pl.ANY)] * len(more),
            out_specs=pl.BlockSpec((1, fb, n, 1, count, D), lambda i, me: (0, i, 0, r0 // count, 0, 0)),
        ),
        out_shape=jax.ShapeDtypeStruct((1, feats, n, each, count, D), F32),
        input_output_aliases={2 + n: 0} if more else {},
        compiler_params=pltpu.CompilerParams(vmem_limit_bytes=VMEM),
        cost_estimate=COST,
        name="final",
    )(me, g.reshape(feats, n, each, count, D), *ds, *more)
    return out.reshape(1, feats, rows, D)


def pack_kernel(*refs):
    vectors, qkv, *mats, down, first, pack = refs
    first[:, :QKV] = qkv[...]
    r = qkv.shape[0]
    first[:, QKV:] = jnp.broadcast_to(vectors[...], (r, 128))
    at = 0
    for m in mats:
        for j in range(m.shape[1] // D):
            pack[at : at + r] = m[:, j * D : (j + 1) * D]
            at += r
    pack[at:] = down[...]


def pack_shards(vectors, qkv, mats, down):
    r = qkv.shape[0]
    if r % ROWS_P:
        pack = jnp.concatenate([m[:, j * D : (j + 1) * D] for m in mats for j in range(m.shape[1] // D)] + [down], axis=0)
        return jnp.concatenate([qkv, jnp.broadcast_to(vectors, (r, 128))], axis=1), pack
    return pl.pallas_call(
        pack_kernel, out_shape=[jax.ShapeDtypeStruct((r, QKV + 128), BF), jax.ShapeDtypeStruct((13 * r, D), BF)], name="pack"
    )(vectors, qkv, *mats, down)


def row_allowed(segments, context):
    tables = jnp.arange(context.shape[0], dtype=jnp.int32)
    member = (segments[:, None] == tables[None, :]).astype(jnp.int32)
    sizes = jnp.sum(member, axis=0)
    starts = jnp.cumsum(sizes) - sizes
    places = jnp.arange(segments.shape[0], dtype=jnp.int32) - jnp.sum(member * starts[None, :], axis=1)
    limits = jnp.sum(member * context[None, :], axis=1)
    usable = places < limits
    return (segments[:, None] == segments[None, :]) & usable[None, :]


def swap(arrays, n):
    return [arrays[0]] + [lax.ppermute(arrays[k], "feat", [(d, d ^ k) for d in range(n)]) for k in range(1, n)]


def exchange(x, me, n):
    feats, rows, _ = x.shape

    def move(a, at, rows, bit):
        low = ((me // bit) % 2) * rows
        sent = lax.dynamic_slice(a, (0, at + rows - low, 0), (feats, rows, D))
        return lax.ppermute(sent, "feat", [(d, d ^ bit) for d in range(n)]), at + low

    bit = n // 2
    got, low = move(x, 0, rows // 2, bit)
    got = [got]

    def finish():
        have, places, half, bit = [(x, low), (got[0], 0)], [0, n // 2], rows // 2, n // 4
        while bit:
            half //= 2
            moved = [move(a, at, half, bit) for a, at in have]
            have = [(a, at) for (a, _), (_, at) in zip(have, moved)] + [(a, 0) for a, _ in moved]
            places = places + [q ^ bit for q in places]
            bit //= 2
        return [have[places.index(k)] for k in range(n)]

    return got, finish


class Shards:
    def __init__(self, rows, n):
        self.count = rows * n
        self.bits = [("rows", 1 << b) for b in reversed(range(rows.bit_length() - 1))]
        self.bits += [("feat", 1 << b) for b in reversed(range(n.bit_length() - 1))]
        self.sizes = {"rows": rows, "feat": n}
        last = len(self.bits) - 1
        self.rows_bits = list(range(rows.bit_length() - 1))
        self.near = last
        self.feat_bits = list(range(rows.bit_length() - 1, last))

    def other(self, a, at):
        axis, bit = self.bits[at]
        return lax.ppermute(a, axis, [(d, d ^ bit) for d in range(self.sizes[axis])])

    def side(self, at):
        axis, bit = self.bits[at]
        return (lax.axis_index(axis) // bit) % 2

    def gather(self, a, order):
        if a.ndim == 2:
            a = a.reshape((1,) * len(self.bits) + a.shape)
        while order:
            at, *rest = order
            if rest and rest[0] == at + 1 and self.bits[at][0] == "rows" == self.bits[at + 1][0] and self.sizes["rows"] <= 8:
                a = self.gather_two(a, at)
                order = rest[1:]
                continue
            b = self.other(a, at)
            low = self.side(at) == 0
            a = jnp.concatenate([jnp.where(low, a, b), jnp.where(low, b, a)], axis=at)
            order = rest
        return a

    def gather_two(self, a, at):
        axis, high = self.bits[at]
        low = self.bits[at + 1][1]
        move = lambda mask: lax.ppermute(a, axis, [(d, d ^ mask) for d in range(self.sizes[axis])])
        all_ = [[a, move(low)], [move(high), move(high | low)]]
        line = lambda q, side: jnp.concatenate([jnp.where(side, q[1], q[0]), jnp.where(side, q[0], q[1])], axis=at + 1)
        q = [line(pair, self.side(at + 1) == 1) for pair in all_]
        side = self.side(at) == 1
        return jnp.concatenate([jnp.where(side, q[1], q[0]), jnp.where(side, q[0], q[1])], axis=at)

    def halve(self, a, at):
        side = self.side(at)
        return [lax.dynamic_index_in_dim(a, i, at, True) for i in (side, 1 - side)]

    def quarter(self, a, at):
        high, low = self.side(at), self.side(at + 1)
        pick = lambda i, j: lax.dynamic_index_in_dim(lax.dynamic_index_in_dim(a, i, at, True), j, at + 1, True)
        return pick(high, low), [pick(high, 1 - low), pick(1 - high, low), pick(1 - high, 1 - low)]

    def others(self, parts, at):
        axis, high = self.bits[at]
        low = self.bits[at + 1][1]
        masks = (low, high, high | low)
        return [lax.ppermute(a, axis, [(d, d ^ mask) for d in range(self.sizes[axis])]) for a, mask in zip(parts, masks)]


def total(terms, held=BF):
    return sum([a.astype(F32) for a in terms[1:]], terms[0].astype(F32)).astype(held)


def begin(shards, sums, ats):
    halves = [shards.halve(a, at) for a, at in zip(sums, ats)]
    return [[mine, shards.other(others, at)] for (mine, others), at in zip(halves, ats)]


def unpack_kernel(*refs, counts):
    na, nb, nc = counts
    ins, outs = refs[: na + nb + nc], refs[na + nb + nc :]
    add = lambda terms, rows, cols=slice(None): sum([t[rows, cols].astype(F32) for t in terms[1:]], terms[0][rows, cols].astype(F32))
    a, b, c = ins[:na], ins[na : na + nb], ins[na + nb :]
    out_one, qkv_two, out_two, up, down, qkv_one, vectors = outs
    r = out_one.shape[0]
    at = 0
    for ref in (out_one, qkv_two, out_two, up):
        for j in range(ref.shape[1] // D):
            terms, row = (a, at) if at < SHARE else (b, at - SHARE)
            ref[:, j * D : (j + 1) * D] = add(terms, slice(row, row + r))
            at += r
    down[...] = add(b, slice(at - SHARE, at - SHARE + down.shape[0]))
    qkv_one[...] = add(c, slice(None), slice(0, QKV))
    vectors[...] = add(c, slice(None), slice(QKV, QKV + 128)).T


def unpack(two, dfirst, r):
    sums = [[a.reshape(a.shape[-2:]) for a in terms] for terms in (*two, dfirst)]
    if r % ROWS_P:
        pack = jnp.concatenate([total(sums[0], F32), total(sums[1], F32)])
        piece = lambda a, b: jnp.concatenate([pack[j * r : (j + 1) * r] for j in range(a, b)], axis=1)
        dfirst = total(sums[2], F32)
        return piece(0, 1), piece(1, 4), piece(4, 5), piece(5, 9), pack[9 * r :], dfirst[:, :QKV], dfirst[:, QKV:].T
    shapes = [(r, D), (r, QKV), (r, D), (r, FF), (4 * r, D), (r, QKV), (128, r)]
    return pl.pallas_call(
        lambda *refs: unpack_kernel(*refs, counts=[len(terms) for terms in sums]),
        out_shape=[jax.ShapeDtypeStruct(q, F32) for q in shapes],
        name="unpack",
    )(*[a for terms in sums for a in terms])


def split_sum(shards, mine, others, core):
    if shards.count == D // ROWS_P:
        terms = [mine, shards.other(others, shards.near)]
        return [a.reshape((2,) * (len(shards.bits) - 1) + (1,) + a.shape[1:]) for a in terms]
    both = jnp.where(core == 0, jnp.stack((mine, others), 1), jnp.stack((others, mine), 1))
    both = both.reshape((D // ROWS_P,) + mine.shape[1:])
    if mine.shape[1] == ROWS_P:
        both = both.reshape(shards.count, -1, both.shape[2])
    else:
        both = repack(both, shards.count)
    return begin(shards, [both.reshape((2,) * len(shards.bits) + both.shape[1:])], [shards.near])[0]


def together(a, b):
    return lax.optimization_barrier((a, b))


def repack(a, blocks):
    count = a.shape[0]
    if count == blocks:
        return a
    r, q = D // count, D // blocks
    parts = [a[:, j * r : (j + 1) * r].reshape(blocks, q, D) for j in range(9)]
    return jnp.concatenate(parts + [a[:, 9 * r :].reshape(blocks, 4 * q, D)], axis=1)


def per_device(rows_axis, n, inputs, *rest):
    weights, (cotangent, segments, context, feature_mask) = rest[:12], rest[12:]
    gain_one, shift_one, qkv_one, out_one, gain_two, shift_two, qkv_two, out_two, gain_three, shift_three, up, down = weights
    shards = Shards(rows_axis, n)
    _, feats, rows, _ = inputs.shape
    part = rows // n
    tot = n * feats
    me = lax.axis_index("feat").astype(jnp.int32)
    me_arr = me.reshape(1)

    core = (me % 2).reshape(1)
    vectors = (gain_one, shift_one, gain_two, shift_two, gain_three, shift_three)
    r = D // shards.count
    vectors = sum(jnp.pad(v, (j * r, 128 - (j + 1) * r)) for j, v in enumerate(vectors)).reshape(1, 128)
    first, pack = pack_shards(vectors, qkv_one, (out_one, qkv_two, out_two, up), down)
    pack = repack(lax.all_gather(pack, ("rows", "feat"), axis=0), D // ROWS_P)
    first = shards.gather(first, shards.feat_bits[:1])
    got, xs_at = exchange(together(inputs, first)[0][0], me, n)
    first = shards.gather(first, shards.feat_bits[1:] + shards.rows_bits)
    got[0], first = together(got[0], first)
    xs_at = xs_at()
    first = shards.gather(first, [shards.near]).reshape(D, QKV + 128)
    gains = first.reshape(shards.count, r, QKV + 128)[:, 0, QKV : QKV + 6 * r].reshape(shards.count, 6, r)
    gains = gains.transpose(1, 0, 2).reshape(6, D).astype(F32)
    g1, b1, g2, b2, g3, b3 = [gains[j : j + 1] for j in range(6)]

    xs = [a for a, _ in xs_at]
    x_rows = jnp.stack([jnp.asarray(at, jnp.int32) // RC for _, at in xs_at] + [core[0]])
    order = me ^ jnp.arange(n, dtype=jnp.int32)
    valid = jnp.take(feature_mask[0].reshape(n, feats), order, axis=0).reshape(tot) > 0
    wide = -(-2 * tot // 128) * 128
    lane = jnp.arange(wide)
    same = (lane[None, :] // tot == jnp.arange(2 * tot)[:, None] // tot) & (lane < 2 * tot)[None, :]
    bias_one = jnp.where(same & jnp.pad(jnp.tile(valid, 2), (0, wide - 2 * tot))[None, :], 0.0, MASKED).astype(F32)
    bias_two = jnp.where(row_allowed(segments[0], context[0]), 0.0, MASKED).astype(F32)

    cut = feats // 3 // FB * FB
    cuts = ((0, cut), (cut, feats))
    half = part // 2
    res = feature_forward(x_rows, xs, g1, b1, first, bias_one, cuts, part)
    qkv, p = res[2 * n :]
    h_a, h_b = swap(res[:n], n), swap(res[n : 2 * n], n)
    gains_two = (g2, b2, g3, b3)
    res = middle(me_arr, core, inputs, h_a, cotangent, bias_two, pack, *gains_two, 0, ((0, part),), [])
    output, gaf, carried = res[0], res[1], res[2 + n :]
    g_a = swap(res[2 : 2 + n], n)
    spans = ((0, half), (half, part))
    res = middle(me_arr, core, inputs, h_b, cotangent, bias_two, pack, *gains_two, cut, spans, [*carried, output, gaf])
    g_a, res = together(g_a, res)
    output, gaf = res[:2]
    g_b, g_c = swap(res[2 : 2 + n], n), swap(res[2 + n : 2 + 2 * n], n)
    mine, others, *vector_grads = res[2 + 2 * n :]

    wide_first, tall_first = shards.rows_bits[::-1], shards.rows_bits[-2::-1] + shards.rows_bits[-1:]
    ways = [way + shards.feat_bits for way in (wide_first, tall_first)]
    on = lambda i: [way[i] for way in ways]
    dpack = total(split_sum(shards, mine, others, core[0]))
    dpack, g_b = together(dpack, g_b)
    share = SHARE if shards.count == D // ROWS_P else dpack.shape[-2] // 2
    two = [dpack[..., :share, :], dpack[..., share:, :]]

    two = begin(shards, two, on(0))
    *d_a, acc, dg1, db1 = feature_backward(
        x_rows, xs, [(0, g_a), (0, g_b)], qkv, p, g1, b1, first, cuts, 0, half, [], []
    )
    two, d_a, g_c = lax.optimization_barrier((two, d_a, g_c))
    two, g_c = together([total(terms) for terms in two], g_c)

    two = begin(shards, two, on(1))
    d_a = swap(d_a, n)
    *d_b, kept, others = feature_backward(
        x_rows, xs, [(0, g_a), (half, g_c)], qkv, p, g1, b1, first, cuts, half, part, [acc, dg1, db1], vector_grads
    )
    two, d_a, d_b, kept, others = lax.optimization_barrier((two, d_a, d_b, kept, others))
    dfirst = total(split_sum(shards, kept, others, core[0]))
    d_b = swap(d_b, n)
    two = [total(terms) for terms in two]
    for i in range(2, len(ways[0]) - 2):
        two = [total(terms) for terms in begin(shards, two, on(i))]
    d_a, dfirst = together(d_a, dfirst)

    *two, dfirst = begin(shards, [*two, dfirst], on(-2) + wide_first[:1])
    input_grad = final(me_arr, gaf, d_a, 0, None)
    two, dfirst, input_grad = lax.optimization_barrier((two, dfirst, input_grad))
    two = begin(shards, [total(terms) for terms in two], on(-1))
    dfirst = total(dfirst)
    last = wide_first[1:] + shards.feat_bits
    if len(last) == 3:
        kept, others = shards.quarter(dfirst, last[1])
        two, others, d_b = lax.optimization_barrier((two, shards.others(others, last[1]), d_b))
        input_grad = final(me_arr, gaf, d_b, half, input_grad)
        two, others, input_grad = lax.optimization_barrier((two, others, input_grad))
        dfirst = total([kept] + others)
        last = last[2:]
    else:
        input_grad = final(me_arr, gaf, d_b, half, input_grad)
    for at in last[:-1]:
        dfirst = total(begin(shards, [dfirst], [at])[0])
    dfirst = begin(shards, [dfirst], last[-1:])[0]
    d_out_one, d_qkv_two, d_out_two, d_up, d_down, d_qkv_one, vectors = unpack(two, dfirst, r)
    v = [vectors[j] for j in range(6)]
    return (output, input_grad, v[0], v[1], d_qkv_one, d_out_one, v[2], v[3], d_qkv_two, d_out_two, v[4], v[5], d_up, d_down)


def solution(mesh):
    rows_axis, n = mesh.shape["rows"], mesh.shape["feat"]
    vec, mat, act, tab = P(("rows", "feat")), P(("rows", "feat"), None), P("rows", "feat", None, None), P("rows", None)
    weights = (vec, vec, mat, mat, vec, vec, mat, mat, vec, vec, mat, mat)
    return jax.shard_map(
        lambda *a: per_device(rows_axis, n, *a),
        mesh=mesh,
        in_specs=(act,) + weights + (act, tab, tab, tab),
        out_specs=(act, act) + weights,
        check_vma=False,
    )
```
